32 devices in a mesh: space: 16 (over z, x, core), event: 2 (over y).
Axes of the slice: x: 2, y: 2, z: 4, core: 2. Of those that a mesh axis runs over, the one named last changes fastest.
Arguments:
- green: bfloat16 [8, 512, 2, 6, 2048], P(None, 'event', None, None, 'space'), may hold values from -6 to 6
- strain: bfloat16 [48, 8, 2, 6, 2048], P('event', None, None, None, 'space'), may hold values from -6 to 6
- perturb: float32 [2048], P('space'), may hold values from -6 to 6
- pairs: int32 [48, 512], P(None, 'event'), may hold values 0 or 1
Outputs:
- hessian: float32 [2048], P(('space', 'event'))
The draws below stay inside these ranges and needn't reach their ends.
All inputs are finite; a program needn't handle non-finite values. No bound on the sum of `pairs` on one device may be relied on, other than what follows from the above.
Results may differ from the reference program's by a relative error of at most 0.00096.
Values may be sent and summed in bfloat16 or wider, within the bound.
A program may use at most 64 MiB of HBM per device.

```python
import math
import jax
import jax.numpy as jnp
from jax import lax

F = 8
R = 512
C = 6
NX = 2048
E = 48


def plant(drawn, rng, least, top_value):
    place = [jax.random.randint(jax.random.fold_in(rng, axis), (), 0, length) for axis, length in enumerate(drawn.shape)]
    main_axis = drawn.shape.index(max(drawn.shape))
    next_to = place[:main_axis] + [(place[main_axis] + 1) % drawn.shape[main_axis]] + place[main_axis + 1:]
    return drawn.at[tuple(place)].set(least).at[tuple(next_to)].set(top_value)


def block_scale(key, dims, cuts, smallest, high):
    loudness, own = 1.0, jax.random.fold_in(key, 6)
    for axis_at, shards_of in cuts:
        draws = jnp.exp(jax.random.uniform(jax.random.fold_in(own, axis_at), (shards_of,), jnp.float32, smallest / len(cuts), high / len(cuts)))
        loudness = loudness * jnp.repeat(draws, dims[axis_at] // shards_of).reshape([-1 if axis == axis_at else 1 for axis in range(len(dims))])
    return loudness


def gaussian(key, extent, deviation, reach, shards=(), kind=jnp.bfloat16):
    entries = jax.random.normal(key, extent, jnp.float32) * deviation
    if len(shards) > 0:
        entries = block_scale(key, extent, shards, -0.22, 0.18) * entries
    return jnp.clip(entries, min=-reach, max=reach).astype(kind)


def setup_inputs(seed: int = 0) -> dict:
    key_of = jax.random.split(jax.random.key(seed), 5)
    green = gaussian(key_of[0], (F, R, 2, C, NX), 1.0, 6.0, ((1, 2), (4, 16)))
    strain = gaussian(key_of[1], (E, F, 2, C, NX), 1.0, 6.0, ((0, 2), (4, 16)))
    perturb = gaussian(key_of[2], (NX,), 1.0, 6.0, ((0, 16),), jnp.float32)
    pairs = plant((jax.random.randint(key_of[3], (E, R), 0, 4) < 3).astype(jnp.int32), jax.random.fold_in(key_of[3], 1), 0, 1)
    return dict(green=green, strain=strain, perturb=perturb, pairs=pairs)


def one_frequency(green_f, strain_f, perturb, mask, scale_one):
    events = strain_f.shape[0]
    receivers = green_f.shape[0]
    weighted = (strain_f.astype(jnp.float32) * perturb).astype(jnp.bfloat16)
    w_real = weighted[:, 0].reshape(events, -1)
    w_imag = weighted[:, 1].reshape(events, -1)
    combo = jnp.stack([jnp.stack([w_real, -w_imag], 1), jnp.stack([w_imag, w_real], 1)], 0)
    flat_green = green_f.reshape(receivers, 2, -1).astype(jnp.float32)
    data = scale_one * jnp.einsum('rpk,qepk->qer', flat_green, combo.astype(jnp.float32))
    resid = (data * mask[None]).astype(jnp.bfloat16)
    back_in = jnp.stack([jnp.stack([resid[0], resid[1]], 1), jnp.stack([resid[1], -resid[0]], 1)], 0)
    back = jnp.einsum('qepr,rpk->qek', back_in.astype(jnp.float32), flat_green)
    flat_strain = strain_f.reshape(events, 2, -1).astype(jnp.float32)
    terms = jnp.einsum('qek,eqk->k', back, flat_strain)
    return terms.reshape(strain_f.shape[2], -1).sum(0)

def reference(green, strain, perturb, pairs):
    freqs = green.shape[0]
    cells = perturb.shape[0]
    events = strain.shape[0]
    receivers = green.shape[1]
    scale_one = 1.0 / math.sqrt(12.0 * cells)
    scale_two = 1.0 / math.sqrt(12.0 * events * freqs * receivers)
    mask = pairs.astype(jnp.float32)
    strain_by_freq = jnp.moveaxis(strain, 1, 0)

    def step(total, items):
        green_f, strain_f = items
        return (total + one_frequency(green_f, strain_f, perturb, mask, scale_one), None)
    total, unused = lax.scan(step, jnp.zeros((cells,), jnp.float32), (green, strain_by_freq))
    return scale_two * total
```

```python
import functools
import math

import jax
import jax.numpy as jnp
from jax import lax
from jax.experimental import pallas as pl
from jax.experimental.pallas import tpu as pltpu
from jax.sharding import PartitionSpec as P

MESH = pl.DeviceIdType.MESH
F32 = jnp.float32
BF16 = jnp.bfloat16


def kernel(
    n_space, n_event, inner, freqs, recv, comps, cells, events,
    green_ref, strain_ref, perturb_ref, pairs_ref, out_ref,
    raw_green, raw_strain, wide_green, wide_strain, g, s, part, got1, half, got2, res, acc, ends,
    load_sem, strain_s, strain_r, rs1_s, rs1_r, rs2_s, rs2_r, ag2_s, ag2_r, ag1_s, ag1_r, end_s, end_r,
):
    outer = n_space // inner
    tiles = recv // 128
    per_inner = freqs * tiles // inner
    per_part = freqs // inner
    rows = 2 * comps
    scale_one = 1.0 / math.sqrt(12.0 * cells * n_space)
    scale_two = 1.0 / math.sqrt(12.0 * events * n_event * freqs * recv * n_event)

    me = lax.axis_index("space")
    y = lax.axis_index("event")
    i = lax.rem(me, inner)
    o = lax.div(me, inner)

    def at_event(d):
        return {"event": lax.rem(y + d + n_event, n_event)}

    def at_inner(d):
        return {"space": o * inner + lax.rem(i + d + inner, inner)}

    def at_outer(d):
        return {"space": lax.rem(o + d + outer, outer) * inner + i}

    def remote(src, dst, send, recv_, device):
        return pltpu.make_async_remote_copy(
            src_ref=src, dst_ref=dst, send_sem=send, recv_sem=recv_, device_id=device, device_id_type=MESH
        )

    def when(cond, fn):
        if per_inner == outer:
            fn()
        else:
            pl.when(cond)(fn)

    strain_load = pltpu.make_async_copy(strain_ref, raw_strain, load_sem.at[freqs])
    strain_load.start()

    def order(k):
        return lax.rem((i + 1) * per_part + k, freqs)

    def green_load(f):
        return pltpu.make_async_copy(green_ref.at[f], raw_green.at[f], load_sem.at[f])

    for k in range(freqs):
        green_load(order(k)).start()

    barrier = pltpu.get_barrier_semaphore()
    for d in range(1, n_event):
        pl.semaphore_signal(barrier, inc=1, device_id=at_event(d), device_id_type=MESH)
    for d in range(1, inner):
        pl.semaphore_signal(barrier, inc=1, device_id=at_inner(d), device_id_type=MESH)
    for d in range(1, outer):
        pl.semaphore_signal(barrier, inc=1, device_id=at_outer(d), device_id_type=MESH)

    strain_load.wait()
    wide_strain[...] = raw_strain[...].astype(F32)
    pl.semaphore_wait(barrier, n_event + inner + outer - 3)

    def strain_copy(j, f):
        return remote(s.at[0, f], s.at[j, f], strain_s.at[j - 1, f], strain_r.at[j - 1, f], at_event(-j))

    def arrange_strain(k, carry):
        f = order(k)
        for c in range(comps):
            pieces = [
                wide_strain[pl.ds(f * rows + 2 * c + q, events, stride=freqs * rows), :] for q in range(2)
            ]
            s[0, f, :, c * cells:(c + 1) * cells] = jnp.concatenate(pieces, 0).astype(BF16)
        for j in range(1, n_event):
            strain_copy(j, f).start()
        return carry

    lax.fori_loop(0, freqs, arrange_strain, None)

    perturb = jnp.concatenate([perturb_ref[...]] * comps, 1)

    def forward(j, k, arrange):
        def one(n, carry):
            f = order(k * per_part + n)
            if arrange:
                green_load(f).wait()
                wide_green[...] = raw_green[f].astype(F32)
                for c in range(comps):
                    for p in range(2):
                        g[f, p * recv:(p + 1) * recv, c * cells:(c + 1) * cells] = wide_green[
                            pl.ds(2 * c + p, recv, stride=rows), :
                        ].astype(BF16)
            if j > 0:
                for step in range(j, j + 1):
                    strain_copy(step, f).wait_recv()
            weighted = (s[j, f].astype(F32) * perturb).astype(BF16)
            both = lax.dot_general(weighted, g[f], (((1,), (1,)), ((), ())), preferred_element_type=F32)
            real = both[:events, :recv] - both[events:, recv:]
            imag = both[events:, :recv] + both[:events, recv:]
            data = jnp.concatenate([real, imag], 0).astype(BF16)
            for t in range(tiles):
                part[j, f * tiles + t] = data[:, t * 128:(t + 1) * 128]
            return carry

        lax.fori_loop(0, per_part, one, None)
        if k < inner - 1:
            rs1_copy(j, k + 1).start()

    def rs1_copy(j, d):
        target = lax.rem(i + d, inner)
        return remote(
            part.at[j, pl.ds(target * per_inner, per_inner)], got1.at[j, d - 1],
            rs1_s.at[j, d - 1], rs1_r.at[j, d - 1], at_inner(d),
        )

    def rs2_copy(j, d):
        target = lax.rem(o + d, outer)
        return remote(half.at[j, target], got2.at[j, d - 1], rs2_s.at[j, d - 1], rs2_r.at[j, d - 1], at_outer(d))

    def rs2_sends(d):
        return lax.rem(o + d, outer) < per_inner

    def ag2_copy(j, d, t):
        spot = res.at[j, i * per_inner + t]
        return remote(spot, spot, ag2_s.at[j, d - 1], ag2_r.at[j, d - 1], at_outer(d))

    def ag1_copy(j, d, which):
        spot = res.at[j, pl.ds(which * per_inner, per_inner)]
        return remote(spot, spot, ag1_s.at[j, d - 1], ag1_r.at[j, d - 1], at_inner(d))

    def stage1(j):
        for d in range(1, inner):
            rs1_copy(j, d).wait_recv()
        for t in range(per_inner):
            total = part[j, i * per_inner + t].astype(F32)
            for d in range(1, inner):
                total += got1[j, d - 1, t].astype(F32)
            half[j, t] = total.astype(BF16)
        for d in range(1, outer):
            when(rs2_sends(d), lambda d=d: rs2_copy(j, d).start())

    def stage2(j):
        def reduce():
            for d in range(1, outer):
                rs2_copy(j, d).wait_recv()
            total = half[j, o].astype(F32)
            for d in range(1, outer):
                total += got2[j, d - 1].astype(F32)
            owner = lax.rem(y + j, n_event)
            mask = pairs_ref[pl.ds(pl.multiple_of(owner * events, 8), events), :].astype(F32)
            tile = lax.rem(o, tiles)
            chosen = mask[:, :128]
            for t in range(1, tiles):
                chosen = jnp.where(tile == t, mask[:, t * 128:(t + 1) * 128], chosen)
            chosen = jnp.concatenate([chosen, chosen], 0)
            res[j, i * per_inner + o] = (scale_one * total * chosen).astype(BF16)
            for d in range(1, outer):
                ag2_copy(j, d, o).start()

        when(o < per_inner, reduce)

    def stage3(j):
        for d in range(1, outer):
            source = lax.rem(o - d + outer, outer)
            when(source < per_inner, lambda d=d, source=source: ag2_copy(j, d, source).wait_recv())
        for d in range(1, inner):
            ag1_copy(j, d, i).start()

    def stage4(j):
        for d in range(1, inner):
            ag1_copy(j, d, lax.rem(i - d + inner, inner)).wait_recv()

    acc[...] = jnp.zeros_like(acc)

    def backward(j, k):
        def one(n, carry):
            f = k * per_part + n
            both = jnp.concatenate([res[j, f * tiles + t].astype(F32) for t in range(tiles)], 1)
            real, imag = both[:events], both[events:]
            left = jnp.concatenate(
                [jnp.concatenate([real, imag], 1), jnp.concatenate([imag, -real], 1)], 0
            ).astype(BF16)
            back = jnp.dot(left, g[f], preferred_element_type=F32)
            terms = back * s[j, f].astype(F32)
            total = terms[:8]
            for r in range(1, 2 * events // 8):
                total += terms[r * 8:(r + 1) * 8]
            acc[...] += total
            return carry

        lax.fori_loop(0, per_part, one, None)

    for k in range(inner):
        forward(0, k, True)
    for j in range(n_event):
        if j + 1 < n_event:
            beside = [functools.partial(forward, j + 1, k, False) for k in range(inner)]
            if j > 0:
                beside += [functools.partial(backward, j - 1, k) for k in range(inner)]
        else:
            beside = [functools.partial(backward, j - 1, k) for k in range(inner)] if j > 0 else []
        stages = [stage1, stage2, stage3, stage4]
        for n, stage in enumerate(stages):
            stage(j)
            if n < 3:
                cut = len(beside) * (n + 1) // 3
                for fn in beside[len(beside) * n // 3:cut]:
                    fn()
    for k in range(inner):
        backward(n_event - 1, k)

    local = acc[:, :cells]
    for c in range(1, comps):
        local += acc[:, c * cells:(c + 1) * cells]
    ends[0] = local

    def end_copy(d):
        return remote(ends.at[0], ends.at[d], end_s.at[d - 1], end_r.at[d - 1], at_event(-d))

    for d in range(1, n_event):
        end_copy(d).start()

    for j in range(1, n_event):
        for f in range(freqs):
            strain_copy(j, f).wait_send()
    for j in range(n_event):
        for d in range(1, inner):
            rs1_copy(j, d).wait_send()
            ag1_copy(j, d, i).wait_send()
        for d in range(1, outer):
            when(rs2_sends(d), lambda d=d, j=j: rs2_copy(j, d).wait_send())
            when(o < per_inner, lambda d=d, j=j: ag2_copy(j, d, o).wait_send())
    for d in range(1, n_event):
        end_copy(d).wait_recv()
    total = ends[0]
    for d in range(1, n_event):
        total += ends[d]
    total = scale_two * jnp.sum(total, axis=0, keepdims=True)
    width = cells // n_event
    mine = total[:, :width]
    for e in range(1, n_event):
        mine = jnp.where(y == e, total[:, e * width:(e + 1) * width], mine)
    out_ref[...] = mine
    for d in range(1, n_event):
        end_copy(d).wait_send()


def body(green, strain, perturb, pairs):
    freqs, recv = green.shape[0], green.shape[1]
    comps, cells = green.shape[3], green.shape[4]
    events = strain.shape[0]
    n_space = lax.axis_size("space")
    n_event = lax.axis_size("event")
    inner = 4
    outer = n_space // inner
    units = freqs * (recv // 128)
    per_inner = units // inner
    rows = 2 * comps
    flat_green = green.transpose(0, 1, 3, 2, 4).reshape(freqs, recv * rows, cells)
    flat_strain = strain.transpose(0, 1, 3, 2, 4).reshape(events * freqs * rows, cells)
    dma = pltpu.SemaphoreType.DMA
    wide = comps * cells
    hess = pl.pallas_call(
        functools.partial(kernel, n_space, n_event, inner, freqs, recv, comps, cells, events),
        out_shape=jax.ShapeDtypeStruct((1, cells // n_event), F32),
        in_specs=[
            pl.BlockSpec(memory_space=pl.ANY),
            pl.BlockSpec(memory_space=pl.ANY),
            pl.BlockSpec(memory_space=pltpu.VMEM),
            pl.BlockSpec(memory_space=pltpu.VMEM),
        ],
        out_specs=pl.BlockSpec(memory_space=pltpu.VMEM),
        scratch_shapes=[
            pltpu.VMEM((freqs, recv * rows, cells), BF16),
            pltpu.VMEM((events * freqs * rows, cells), BF16),
            pltpu.VMEM((recv * rows, cells), F32),
            pltpu.VMEM((events * freqs * rows, cells), F32),
            pltpu.VMEM((freqs, 2 * recv, wide), BF16),
            pltpu.VMEM((n_event, freqs, 2 * events, wide), BF16),
            pltpu.VMEM((n_event, units, 2 * events, 128), BF16),
            pltpu.VMEM((n_event, inner - 1, per_inner, 2 * events, 128), BF16),
            pltpu.VMEM((n_event, per_inner, 2 * events, 128), BF16),
            pltpu.VMEM((n_event, outer - 1, 2 * events, 128), BF16),
            pltpu.VMEM((n_event, units, 2 * events, 128), BF16),
            pltpu.VMEM((8, wide), F32),
            pltpu.VMEM((n_event, 8, cells), F32),
            dma((freqs + 1,)),
            dma((n_event - 1, freqs)),
            dma((n_event - 1, freqs)),
            dma((n_event, inner - 1)),
            dma((n_event, inner - 1)),
            dma((n_event, outer - 1)),
            dma((n_event, outer - 1)),
            dma((n_event, outer - 1)),
            dma((n_event, outer - 1)),
            dma((n_event, inner - 1)),
            dma((n_event, inner - 1)),
            dma((n_event - 1,)),
            dma((n_event - 1,)),
        ],
        compiler_params=pltpu.CompilerParams(
            collective_id=0, has_side_effects=True, vmem_limit_bytes=60 * 1024 * 1024
        ),
    )(flat_green, flat_strain, perturb.reshape(1, cells), pairs)
    return hess.reshape(-1)


def solution(mesh):
    in_specs = (
        P(None, "event", None, None, "space"),
        P("event", None, None, None, "space"),
        P("space"),
        P(None, "event"),
    )
    out_specs = P(("space", "event"))
    return jax.shard_map(body, mesh=mesh, in_specs=in_specs, out_specs=out_specs, check_vma=False)
```

```python
import functools
import math

import jax
import jax.numpy as jnp
from jax import lax
from jax.experimental import pallas as pl
from jax.experimental.pallas import tpu as pltpu
from jax.sharding import PartitionSpec as P

MESH = pl.DeviceIdType.MESH
F32 = jnp.float32
BF16 = jnp.bfloat16


def each(count, fn):
    if count <= 16:
        for n in range(count):
            fn(n)
    else:
        lax.fori_loop(0, count, lambda n, carry: (fn(n), carry)[1], None)


def kernel(
    n_space, n_event, freqs, recv, comps, cells, events,
    green_ref, strain_ref, perturb_ref, pairs_ref, out_ref,
    raw_green, raw_strain, wide_green, wide_strain, g, s, part, got, res, acc, ends,
    load_sem, strain_s, strain_r, rs_s, rs_r, ag_s, ag_r, end_s, end_r,
):
    tiles = recv // 128
    units = freqs * tiles
    rows = 2 * comps
    block = 2 * events
    ahead = min(3, freqs)
    lag = 2
    scale_one = 1.0 / math.sqrt(12.0 * cells * n_space)

    me = lax.axis_index("space")
    y = lax.axis_index("event")
    my_freq = lax.div(me, tiles)

    def at_event(d):
        return {"event": lax.rem(y + d + n_event, n_event)}

    def peer(d):
        return lax.rem(me + 1 + d, n_space)

    def remote(src, dst, send, recv_, device):
        return pltpu.make_async_remote_copy(
            src_ref=src, dst_ref=dst, send_sem=send, recv_sem=recv_, device_id=device, device_id_type=MESH
        )

    def when(cond, fn):
        if units == n_space:
            fn()
        else:
            pl.when(cond)(fn)

    strain_load = pltpu.make_async_copy(strain_ref, raw_strain, load_sem.at[freqs])
    strain_load.start()

    def green_load(f):
        return pltpu.make_async_copy(green_ref.at[f], raw_green.at[f], load_sem.at[f])

    for f in range(freqs):
        green_load(f).start()

    barrier = pltpu.get_barrier_semaphore()
    for d in range(1, n_event):
        pl.semaphore_signal(barrier, inc=1, device_id=at_event(d), device_id_type=MESH)

    def greet(d):
        pl.semaphore_signal(barrier, inc=1, device_id={"space": peer(d)}, device_id_type=MESH)

    each(n_space - 1, greet)

    strain_load.wait()
    wide_strain[...] = raw_strain[...].astype(F32)
    pl.semaphore_wait(barrier, n_event + n_space - 2)

    def strain_copy(j, f):
        return remote(s.at[0, f], s.at[j, f], strain_s.at[j - 1, f], strain_r.at[j - 1, f], at_event(-j))

    def arrange_strain(f):
        for c in range(comps):
            pieces = [
                wide_strain[pl.ds(f * rows + 2 * c + q, events, stride=freqs * rows), :] for q in range(2)
            ]
            s[0, f, :, c * cells:(c + 1) * cells] = jnp.concatenate(pieces, 0).astype(BF16)
        for j in range(1, n_event):
            strain_copy(j, f).start()

    for f in range(ahead):
        arrange_strain(f)

    perturb = jnp.concatenate([perturb_ref[...]] * comps, 1)

    def arrange_green(f):
        green_load(f).wait()
        wide_green[...] = raw_green[f].astype(F32)
        for c in range(comps):
            for p in range(2):
                g[f, p * recv:(p + 1) * recv, c * cells:(c + 1) * cells] = wide_green[
                    pl.ds(2 * c + p, recv, stride=rows), :
                ].astype(BF16)

    def rs_copy(j, unit, source):
        return remote(
            part.at[j, unit], got.at[j, source], rs_s.at[j, unit], rs_r.at[j, source], {"space": unit}
        )

    def ag_copy(j, d, unit):
        spot = res.at[j, unit]
        return remote(spot, spot, ag_s.at[j, d], ag_r.at[j, unit], {"space": peer(d)})

    def forward(j, f):
        weighted = (s[j, f].astype(F32) * perturb).astype(BF16)
        both = lax.dot_general(weighted, g[f], (((1,), (1,)), ((), ())), preferred_element_type=F32)
        real = both[:events, :recv] - both[events:, recv:]
        imag = both[events:, :recv] + both[:events, recv:]
        data = jnp.concatenate([real, imag], 0).astype(BF16)
        for t in range(tiles):
            unit = f * tiles + t
            part[j, unit] = data[:, t * 128:(t + 1) * 128]
            pl.when(me != unit)(lambda unit=unit: rs_copy(j, unit, me).start())

    def reduce(j):
        def wait(d):
            rs_copy(j, me, peer(d)).wait_recv()

        each(n_space - 1, wait)
        total = part[j, me].astype(F32)
        for d in range(n_space - 1):
            total += got[j, peer(d)].astype(F32)
        owner = lax.rem(y + j, n_event)
        mask = pairs_ref[pl.ds(pl.multiple_of(owner * events, 8), events), :].astype(F32)
        tile = lax.rem(me, tiles)
        chosen = mask[:, :128]
        for t in range(1, tiles):
            chosen = jnp.where(tile == t, mask[:, t * 128:(t + 1) * 128], chosen)
        chosen = jnp.concatenate([chosen, chosen], 0)
        res[j, me] = (scale_one * total * chosen).astype(BF16)
        each(n_space - 1, lambda d: ag_copy(j, d, me).start())

    acc[...] = jnp.zeros_like(acc)

    def backward(j, f):
        for t in range(tiles):
            unit = f * tiles + t
            pl.when(me != unit)(lambda unit=unit: ag_copy(j, 0, unit).wait_recv())
        both = jnp.concatenate([res[j, f * tiles + t].astype(F32) for t in range(tiles)], 1)
        real, imag = both[:events], both[events:]
        left = jnp.concatenate(
            [jnp.concatenate([real, imag], 1), jnp.concatenate([imag, -real], 1)], 0
        ).astype(BF16)
        back = jnp.dot(left, g[f], preferred_element_type=F32)
        terms = back * s[j, f].astype(F32)
        total = terms[:8]
        for r in range(1, block // 8):
            total += terms[r * 8:(r + 1) * 8]
        acc[...] += total

    def loop(fn):
        lax.fori_loop(0, freqs, lambda f, carry: (fn(f), carry)[1], None)

    def first(f):
        arrange_green(f)
        forward(0, f)
        pl.when(f + ahead < freqs)(lambda: arrange_strain(f + ahead))

    def reduce_at(j, step):
        when(me < units, lambda: pl.when(step == my_freq + lag)(lambda: reduce(j)))

    loop(first)
    when(me < units, lambda: reduce(0))
    for j in range(1, n_event):
        def following(f, j=j):
            for q in range(j, j + 1):
                strain_copy(q, f).wait_recv()
            forward(j, f)
            reduce_at(j, f)

        loop(following)

        def between(f, j=j):
            reduce_at(j, f + freqs)
            backward(j - 1, f)

        loop(between)
    loop(lambda f: backward(n_event - 1, f))

    local = acc[:, :cells]
    for c in range(1, comps):
        local += acc[:, c * cells:(c + 1) * cells]
    ends[0] = local

    def end_copy(d):
        return remote(ends.at[0], ends.at[d], end_s.at[d - 1], end_r.at[d - 1], at_event(-d))

    for d in range(1, n_event):
        end_copy(d).start()

    for j in range(1, n_event):
        for f in range(freqs):
            strain_copy(j, f).wait_send()
    for j in range(n_event):
        def sent(unit, j=j):
            pl.when(me != unit)(lambda: rs_copy(j, unit, me).wait_send())

        each(units, sent)
        when(me < units, lambda j=j: each(n_space - 1, lambda d: ag_copy(j, d, me).wait_send()))
    for d in range(1, n_event):
        end_copy(d).wait_recv()
    total = ends[0]
    for d in range(1, n_event):
        total += ends[d]
    total = jnp.sum(total, axis=0, keepdims=True)
    width = cells // n_event
    mine = total[:, :width]
    for e in range(1, n_event):
        mine = jnp.where(y == e, total[:, e * width:(e + 1) * width], mine)
    out_ref[...] = mine
    for d in range(1, n_event):
        end_copy(d).wait_send()


def body(green, strain, perturb, pairs):
    freqs, recv = green.shape[0], green.shape[1]
    comps, cells = green.shape[3], green.shape[4]
    events = strain.shape[0]
    n_space = lax.axis_size("space")
    n_event = lax.axis_size("event")
    units = freqs * (recv // 128)
    rows = 2 * comps
    scale_two = 1.0 / math.sqrt(12.0 * events * n_event * freqs * recv * n_event)
    flat_green = green.transpose(0, 1, 3, 2, 4).reshape(freqs, recv * rows, cells)
    flat_strain = strain.transpose(0, 1, 3, 2, 4).reshape(events * freqs * rows, cells)
    dma = pltpu.SemaphoreType.DMA
    wide = comps * cells
    hess = pl.pallas_call(
        functools.partial(kernel, n_space, n_event, freqs, recv, comps, cells, events),
        out_shape=jax.ShapeDtypeStruct((1, cells // n_event), F32),
        in_specs=[
            pl.BlockSpec(memory_space=pl.ANY),
            pl.BlockSpec(memory_space=pl.ANY),
            pl.BlockSpec(memory_space=pltpu.VMEM),
            pl.BlockSpec(memory_space=pltpu.VMEM),
        ],
        out_specs=pl.BlockSpec(memory_space=pltpu.VMEM),
        scratch_shapes=[
            pltpu.VMEM((freqs, recv * rows, cells), BF16),
            pltpu.VMEM((events * freqs * rows, cells), BF16),
            pltpu.VMEM((recv * rows, cells), F32),
            pltpu.VMEM((events * freqs * rows, cells), F32),
            pltpu.VMEM((freqs, 2 * recv, wide), BF16),
            pltpu.VMEM((n_event, freqs, 2 * events, wide), BF16),
            pltpu.VMEM((n_event, units, 2 * events, 128), BF16),
            pltpu.VMEM((n_event, n_space, 2 * events, 128), BF16),
            pltpu.VMEM((n_event, units, 2 * events, 128), BF16),
            pltpu.VMEM((8, wide), F32),
            pltpu.VMEM((n_event, 8, cells), F32),
            dma((freqs + 1,)),
            dma((n_event - 1, freqs)),
            dma((n_event - 1, freqs)),
            dma((n_event, units)),
            dma((n_event, n_space)),
            dma((n_event, n_space - 1)),
            dma((n_event, units)),
            dma((n_event - 1,)),
            dma((n_event - 1,)),
        ],
        compiler_params=pltpu.CompilerParams(
            collective_id=0, has_side_effects=True, vmem_limit_bytes=60 * 1024 * 1024
        ),
    )(flat_green, flat_strain, perturb.reshape(1, cells), pairs)
    return hess.reshape(-1) * scale_two


def solution(mesh):
    in_specs = (
        P(None, "event", None, None, "space"),
        P("event", None, None, None, "space"),
        P("space"),
        P(None, "event"),
    )
    out_specs = P(("space", "event"))
    return jax.shard_map(body, mesh=mesh, in_specs=in_specs, out_specs=out_specs, check_vma=False)
```

```python
import functools
import math

import jax
import jax.numpy as jnp
from jax import lax
from jax.experimental import pallas as pl
from jax.experimental.pallas import tpu as pltpu
from jax.sharding import PartitionSpec as P

MESH = pl.DeviceIdType.MESH
F32 = jnp.float32
BF16 = jnp.bfloat16


def kernel(
    n_space, n_event, inner, freqs, recv, comps, cells, events,
    green_ref, strain_ref, perturb_ref, pairs_ref, out_ref,
    raw_green, raw_strain, wide_green, wide_strain, g, s, part, got1, half, got2, res, acc, ends,
    load_sem, strain_s, strain_r, rs1_s, rs1_r, rs2_s, rs2_r, ag2_s, ag2_r, ag1_s, ag1_r, end_s, end_r,
):
    outer = n_space // inner
    tiles = recv // 128
    per_inner = freqs * tiles // inner
    per_part = freqs // inner
    rows = 2 * comps
    scale_one = 1.0 / math.sqrt(12.0 * cells * n_space)
    scale_two = 1.0 / math.sqrt(12.0 * events * n_event * freqs * recv * n_event)

    me = lax.axis_index("space")
    y = lax.axis_index("event")
    i = lax.rem(me, inner)
    o = lax.div(me, inner)

    def at_event(d):
        return {"event": lax.rem(y + d + n_event, n_event)}

    def at_inner(d):
        return {"space": o * inner + lax.rem(i + d + inner, inner)}

    def at_outer(d):
        return {"space": lax.rem(o + d + outer, outer) * inner + i}

    def remote(src, dst, send, recv_, device):
        return pltpu.make_async_remote_copy(
            src_ref=src, dst_ref=dst, send_sem=send, recv_sem=recv_, device_id=device, device_id_type=MESH
        )

    def when(cond, fn):
        if per_inner == outer:
            fn()
        else:
            pl.when(cond)(fn)

    strain_load = pltpu.make_async_copy(strain_ref, raw_strain, load_sem.at[freqs])
    strain_load.start()

    def order(k):
        return lax.rem((i + 1) * per_part + k, freqs)

    def green_load(f):
        return pltpu.make_async_copy(green_ref.at[f], raw_green.at[f], load_sem.at[f])

    for k in range(freqs):
        green_load(order(k)).start()

    barrier = pltpu.get_barrier_semaphore()
    for d in range(1, n_event):
        pl.semaphore_signal(barrier, inc=1, device_id=at_event(d), device_id_type=MESH)
    for d in range(1, inner):
        pl.semaphore_signal(barrier, inc=1, device_id=at_inner(d), device_id_type=MESH)
    for d in range(1, outer):
        pl.semaphore_signal(barrier, inc=1, device_id=at_outer(d), device_id_type=MESH)

    strain_load.wait()
    wide_strain[...] = raw_strain[...].astype(F32)
    pl.semaphore_wait(barrier, n_event + inner + outer - 3)

    def strain_copy(j, f):
        return remote(s.at[0, f], s.at[j, f], strain_s.at[j - 1, f], strain_r.at[j - 1, f], at_event(-j))

    def arrange_strain(k, carry):
        f = order(k)
        for c in range(comps):
            pieces = [
                wide_strain[pl.ds(f * rows + 2 * c + q, events, stride=freqs * rows), :] for q in range(2)
            ]
            s[0, f, :, c * cells:(c + 1) * cells] = jnp.concatenate(pieces, 0).astype(BF16)
        for j in range(1, n_event):
            strain_copy(j, f).start()
        return carry

    ahead = min(2, freqs)
    lax.fori_loop(0, ahead, arrange_strain, None)

    perturb = jnp.concatenate([perturb_ref[...]] * comps, 1)

    def forward(j, k, arrange):
        def one(n, carry):
            f = order(k * per_part + n)
            if arrange:
                green_load(f).wait()
                wide_green[...] = raw_green[f].astype(F32)
                for c in range(comps):
                    for p in range(2):
                        g[f, p * recv:(p + 1) * recv, c * cells:(c + 1) * cells] = wide_green[
                            pl.ds(2 * c + p, recv, stride=rows), :
                        ].astype(BF16)
            if j > 0:
                for step in range(j, j + 1):
                    strain_copy(step, f).wait_recv()
            weighted = (s[j, f].astype(F32) * perturb).astype(BF16)
            both = lax.dot_general(weighted, g[f], (((1,), (1,)), ((), ())), preferred_element_type=F32)
            real = both[:events, :recv] - both[events:, recv:]
            imag = both[events:, :recv] + both[:events, recv:]
            data = jnp.concatenate([real, imag], 0).astype(BF16)
            for t in range(tiles):
                part[j, f * tiles + t] = data[:, t * 128:(t + 1) * 128]
            if arrange:
                step = k * per_part + n + ahead
                pl.when(step < freqs)(lambda: arrange_strain(step, None))
            return carry

        lax.fori_loop(0, per_part, one, None)
        if k < inner - 1:
            rs1_copy(j, k + 1).start()

    def rs1_copy(j, d):
        target = lax.rem(i + d, inner)
        return remote(
            part.at[j, pl.ds(target * per_inner, per_inner)], got1.at[j, d - 1],
            rs1_s.at[j, d - 1], rs1_r.at[j, d - 1], at_inner(d),
        )

    def rs2_copy(j, d):
        target = lax.rem(o + d, outer)
        return remote(half.at[j, target], got2.at[j, d - 1], rs2_s.at[j, d - 1], rs2_r.at[j, d - 1], at_outer(d))

    def rs2_sends(d):
        return lax.rem(o + d, outer) < per_inner

    def ag2_copy(j, d, t):
        spot = res.at[j, i * per_inner + t]
        return remote(spot, spot, ag2_s.at[j, d - 1], ag2_r.at[j, d - 1], at_outer(d))

    def ag1_copy(j, d, which):
        spot = res.at[j, pl.ds(which * per_inner, per_inner)]
        return remote(spot, spot, ag1_s.at[j, d - 1], ag1_r.at[j, d - 1], at_inner(d))

    def stage1(j):
        for d in range(1, inner):
            rs1_copy(j, d).wait_recv()
        for t in range(per_inner):
            total = part[j, i * per_inner + t].astype(F32)
            for d in range(1, inner):
                total += got1[j, d - 1, t].astype(F32)
            half[j, t] = total.astype(BF16)
        for d in range(1, outer):
            when(rs2_sends(d), lambda d=d: rs2_copy(j, d).start())

    def stage2(j):
        def reduce():
            for d in range(1, outer):
                rs2_copy(j, d).wait_recv()
            total = half[j, o].astype(F32)
            for d in range(1, outer):
                total += got2[j, d - 1].astype(F32)
            owner = lax.rem(y + j, n_event)
            mask = pairs_ref[pl.ds(pl.multiple_of(owner * events, 8), events), :].astype(F32)
            tile = lax.rem(o, tiles)
            chosen = mask[:, :128]
            for t in range(1, tiles):
                chosen = jnp.where(tile == t, mask[:, t * 128:(t + 1) * 128], chosen)
            chosen = jnp.concatenate([chosen, chosen], 0)
            res[j, i * per_inner + o] = (scale_one * total * chosen).astype(BF16)
            for d in range(1, outer):
                ag2_copy(j, d, o).start()

        when(o < per_inner, reduce)

    def stage3(j):
        for d in range(1, outer):
            source = lax.rem(o - d + outer, outer)
            when(source < per_inner, lambda d=d, source=source: ag2_copy(j, d, source).wait_recv())
        for d in range(1, inner):
            ag1_copy(j, d, i).start()

    acc[...] = jnp.zeros_like(acc)

    def backward(j, k):
        from_inner = lax.rem(i - k + inner, inner)
        if k > 0:
            ag1_copy(j, k, from_inner).wait_recv()

        def one(n, carry):
            f = from_inner * per_part + n
            both = jnp.concatenate([res[j, f * tiles + t].astype(F32) for t in range(tiles)], 1)
            real, imag = both[:events], both[events:]
            left = jnp.concatenate(
                [jnp.concatenate([real, imag], 1), jnp.concatenate([imag, -real], 1)], 0
            ).astype(BF16)
            back = jnp.dot(left, g[f], preferred_element_type=F32)
            terms = back * s[j, f].astype(F32)
            total = terms[:8]
            for r in range(1, 2 * events // 8):
                total += terms[r * 8:(r + 1) * 8]
            acc[...] += total
            return carry

        lax.fori_loop(0, per_part, one, None)

    for k in range(inner):
        forward(0, k, True)
    for j in range(n_event):
        if j + 1 < n_event:
            beside = [functools.partial(forward, j + 1, k, False) for k in range(inner)]
            if j > 0:
                beside += [functools.partial(backward, j - 1, k) for k in range(inner)]
        else:
            beside = [functools.partial(backward, j - 1, k) for k in range(inner)] if j > 0 else []
        for n, stage in enumerate([stage1, stage2, stage3]):
            stage(j)
            if n < 2 or j + 1 < n_event:
                cut = len(beside) * (n + 1) // (3 if j + 1 < n_event else 2)
                for fn in beside[len(beside) * n // (3 if j + 1 < n_event else 2):cut]:
                    fn()
    for k in range(inner):
        backward(n_event - 1, k)

    local = acc[:, :cells]
    for c in range(1, comps):
        local += acc[:, c * cells:(c + 1) * cells]
    ends[0] = local

    def end_copy(d):
        return remote(ends.at[0], ends.at[d], end_s.at[d - 1], end_r.at[d - 1], at_event(-d))

    for d in range(1, n_event):
        end_copy(d).start()

    for j in range(1, n_event):
        for f in range(freqs):
            strain_copy(j, f).wait_send()
    for j in range(n_event):
        for d in range(1, inner):
            rs1_copy(j, d).wait_send()
            ag1_copy(j, d, i).wait_send()
        for d in range(1, outer):
            when(rs2_sends(d), lambda d=d, j=j: rs2_copy(j, d).wait_send())
            when(o < per_inner, lambda d=d, j=j: ag2_copy(j, d, o).wait_send())
    for d in range(1, n_event):
        end_copy(d).wait_recv()
    total = ends[0]
    for d in range(1, n_event):
        total += ends[d]
    total = scale_two * jnp.sum(total, axis=0, keepdims=True)
    width = cells // n_event
    mine = total[:, :width]
    for e in range(1, n_event):
        mine = jnp.where(y == e, total[:, e * width:(e + 1) * width], mine)
    out_ref[...] = mine
    for d in range(1, n_event):
        end_copy(d).wait_send()


def body(green, strain, perturb, pairs):
    freqs, recv = green.shape[0], green.shape[1]
    comps, cells = green.shape[3], green.shape[4]
    events = strain.shape[0]
    n_space = lax.axis_size("space")
    n_event = lax.axis_size("event")
    inner = 4
    outer = n_space // inner
    units = freqs * (recv // 128)
    per_inner = units // inner
    rows = 2 * comps
    flat_green = green.transpose(0, 1, 3, 2, 4).reshape(freqs, recv * rows, cells)
    flat_strain = strain.transpose(0, 1, 3, 2, 4).reshape(events * freqs * rows, cells)
    dma = pltpu.SemaphoreType.DMA
    wide = comps * cells
    hess = pl.pallas_call(
        functools.partial(kernel, n_space, n_event, inner, freqs, recv, comps, cells, events),
        out_shape=jax.ShapeDtypeStruct((1, cells // n_event), F32),
        in_specs=[
            pl.BlockSpec(memory_space=pl.ANY),
            pl.BlockSpec(memory_space=pl.ANY),
            pl.BlockSpec(memory_space=pltpu.VMEM),
            pl.BlockSpec(memory_space=pltpu.VMEM),
        ],
        out_specs=pl.BlockSpec(memory_space=pltpu.VMEM),
        scratch_shapes=[
            pltpu.VMEM((freqs, recv * rows, cells), BF16),
            pltpu.VMEM((events * freqs * rows, cells), BF16),
            pltpu.VMEM((recv * rows, cells), F32),
            pltpu.VMEM((events * freqs * rows, cells), F32),
            pltpu.VMEM((freqs, 2 * recv, wide), BF16),
            pltpu.VMEM((n_event, freqs, 2 * events, wide), BF16),
            pltpu.VMEM((n_event, units, 2 * events, 128), BF16),
            pltpu.VMEM((n_event, inner - 1, per_inner, 2 * events, 128), BF16),
            pltpu.VMEM((n_event, per_inner, 2 * events, 128), BF16),
            pltpu.VMEM((n_event, outer - 1, 2 * events, 128), BF16),
            pltpu.VMEM((n_event, units, 2 * events, 128), BF16),
            pltpu.VMEM((8, wide), F32),
            pltpu.VMEM((n_event, 8, cells), F32),
            dma((freqs + 1,)),
            dma((n_event - 1, freqs)),
            dma((n_event - 1, freqs)),
            dma((n_event, inner - 1)),
            dma((n_event, inner - 1)),
            dma((n_event, outer - 1)),
            dma((n_event, outer - 1)),
            dma((n_event, outer - 1)),
            dma((n_event, outer - 1)),
            dma((n_event, inner - 1)),
            dma((n_event, inner - 1)),
            dma((n_event - 1,)),
            dma((n_event - 1,)),
        ],
        compiler_params=pltpu.CompilerParams(
            collective_id=0, has_side_effects=True, vmem_limit_bytes=60 * 1024 * 1024
        ),
    )(flat_green, flat_strain, perturb.reshape(1, cells), pairs)
    return hess.reshape(-1)


def solution(mesh):
    in_specs = (
        P(None, "event", None, None, "space"),
        P("event", None, None, None, "space"),
        P("space"),
        P(None, "event"),
    )
    out_specs = P(("space", "event"))
    return jax.shard_map(body, mesh=mesh, in_specs=in_specs, out_specs=out_specs, check_vma=False)
```

```python
import functools
import math

import jax
import jax.numpy as jnp
from jax import lax
from jax.experimental import pallas as pl
from jax.experimental.pallas import tpu as pltpu
from jax.sharding import PartitionSpec as P

MESH = pl.DeviceIdType.MESH
F32 = jnp.float32
BF16 = jnp.bfloat16


def kernel(
    n_space, n_event, inner, freqs, recv, comps, cells, events,
    green_ref, strain_ref, perturb_ref, pairs_ref, out_ref,
    raw_green, raw_strain, wide_green, wide_strain, g, s, part, got1, half, got2, res, acc, ends,
    load_sem, strain_s, strain_r, rs1_s, rs1_r, rs2_s, rs2_r, ag2_s, ag2_r, ag1_s, ag1_r, end_s, end_r,
):
    outer = n_space // inner
    tiles = recv // 128
    per_inner = freqs * tiles // inner
    per_part = freqs // inner
    rows = 2 * comps
    scale_one = 1.0 / math.sqrt(12.0 * cells * n_space)
    scale_two = 1.0 / math.sqrt(12.0 * events * n_event * freqs * recv * n_event)

    me = lax.axis_index("space")
    y = lax.axis_index("event")
    i = lax.rem(me, inner)
    o = lax.div(me, inner)

    def at_event(d):
        return {"event": lax.rem(y + d + n_event, n_event)}

    def at_inner(d):
        return {"space": o * inner + lax.rem(i + d + inner, inner)}

    def at_outer(d):
        return {"space": lax.rem(o + d + outer, outer) * inner + i}

    def remote(src, dst, send, recv_, device):
        return pltpu.make_async_remote_copy(
            src_ref=src, dst_ref=dst, send_sem=send, recv_sem=recv_, device_id=device, device_id_type=MESH
        )

    def when(cond, fn):
        if per_inner == outer:
            fn()
        else:
            pl.when(cond)(fn)

    strain_load = pltpu.make_async_copy(strain_ref, raw_strain, load_sem.at[freqs])
    strain_load.start()

    def order(k):
        return lax.rem((i + 1) * per_part + k, freqs)

    def green_load(f):
        return pltpu.make_async_copy(green_ref.at[f], raw_green.at[f], load_sem.at[f])

    for k in range(freqs):
        green_load(order(k)).start()

    barrier = pltpu.get_barrier_semaphore()
    for d in range(1, n_event):
        pl.semaphore_signal(barrier, inc=1, device_id=at_event(d), device_id_type=MESH)
    for d in range(1, inner):
        pl.semaphore_signal(barrier, inc=1, device_id=at_inner(d), device_id_type=MESH)
    for d in range(1, outer):
        pl.semaphore_signal(barrier, inc=1, device_id=at_outer(d), device_id_type=MESH)

    strain_load.wait()
    wide_strain[...] = raw_strain[...].astype(F32)
    pl.semaphore_wait(barrier, n_event + inner + outer - 3)

    def strain_copy(j, f):
        return remote(s.at[0, f], s.at[j, f], strain_s.at[j - 1, f], strain_r.at[j - 1, f], at_event(-j))

    def arrange_strain(k, carry):
        f = order(k)
        for c in range(comps):
            pieces = [
                wide_strain[pl.ds(f * rows + 2 * c + q, events, stride=freqs * rows), :] for q in range(2)
            ]
            s[0, f, :, c * cells:(c + 1) * cells] = jnp.concatenate(pieces, 0).astype(BF16)
        return carry

    def send_strain(k):
        for j in range(1, n_event):
            strain_copy(j, order(k)).start()

    ahead = min(2, freqs)
    for k in range(ahead):
        arrange_strain(k, None)
        send_strain(k)

    perturb = jnp.concatenate([perturb_ref[...]] * comps, 1)

    def forward(j, k, arrange):
        def one(n, carry):
            f = order(k * per_part + n)
            if arrange:
                green_load(f).wait()
                wide_green[...] = raw_green[f].astype(F32)
                for c in range(comps):
                    for p in range(2):
                        g[f, p * recv:(p + 1) * recv, c * cells:(c + 1) * cells] = wide_green[
                            pl.ds(2 * c + p, recv, stride=rows), :
                        ].astype(BF16)
            if j > 0:
                for step in range(j, j + 1):
                    strain_copy(step, f).wait_recv()
            weighted = s[j, f].astype(F32) * perturb
            swapped = jnp.concatenate([-weighted[events:], weighted[:events]], 0)
            along = (((1,), (1,)), ((), ()))
            data = lax.dot_general(g[f, :recv], weighted.astype(BF16), along, preferred_element_type=F32)
            data += lax.dot_general(g[f, recv:], swapped.astype(BF16), along, preferred_element_type=F32)
            data = data.T.astype(BF16)
            for t in range(tiles):
                part[j, f * tiles + t] = data[:, t * 128:(t + 1) * 128]
            if arrange:
                step = k * per_part + n
                pl.when(step + ahead < freqs)(lambda: arrange_strain(step + ahead, None))
                pl.when(lax.rem(step, 2) == 1)(lambda: send_strain(ahead + lax.div(step, 2)))
            return carry

        lax.fori_loop(0, per_part, one, None)
        if k < inner - 1:
            rs1_copy(j, k + 1).start()

    def rs1_copy(j, d):
        target = lax.rem(i + d, inner)
        return remote(
            part.at[j, pl.ds(target * per_inner, per_inner)], got1.at[j, d - 1],
            rs1_s.at[j, d - 1], rs1_r.at[j, d - 1], at_inner(d),
        )

    def rs2_copy(j, d):
        target = lax.rem(o + d, outer)
        return remote(half.at[j, target], got2.at[j, d - 1], rs2_s.at[j, d - 1], rs2_r.at[j, d - 1], at_outer(d))

    def rs2_sends(d):
        return lax.rem(o + d, outer) < per_inner

    def ag2_copy(j, d, t):
        spot = res.at[j, i * per_inner + t]
        return remote(spot, spot, ag2_s.at[j, d - 1], ag2_r.at[j, d - 1], at_outer(d))

    def ag1_copy(j, d, which):
        spot = res.at[j, pl.ds(which * per_inner, per_inner)]
        return remote(spot, spot, ag1_s.at[j, d - 1], ag1_r.at[j, d - 1], at_inner(d))

    def stage1(j):
        for d in range(1, inner):
            rs1_copy(j, d).wait_recv()
        for t in range(per_inner):
            total = part[j, i * per_inner + t].astype(F32)
            for d in range(1, inner):
                total += got1[j, d - 1, t].astype(F32)
            half[j, t] = total.astype(BF16)
        for d in range(1, outer):
            when(rs2_sends(d), lambda d=d: rs2_copy(j, d).start())

    def stage2(j):
        def reduce():
            for d in range(1, outer):
                rs2_copy(j, d).wait_recv()
            total = half[j, o].astype(F32)
            for d in range(1, outer):
                total += got2[j, d - 1].astype(F32)
            owner = lax.rem(y + j, n_event)
            mask = pairs_ref[pl.ds(pl.multiple_of(owner * events, 8), events), :].astype(F32)
            tile = lax.rem(o, tiles)
            chosen = mask[:, :128]
            for t in range(1, tiles):
                chosen = jnp.where(tile == t, mask[:, t * 128:(t + 1) * 128], chosen)
            chosen = jnp.concatenate([chosen, chosen], 0)
            res[j, i * per_inner + o] = (scale_one * total * chosen).astype(BF16)
            for d in range(1, outer):
                ag2_copy(j, d, o).start()

        when(o < per_inner, reduce)

    def stage3(j):
        for d in range(1, outer):
            source = lax.rem(o - d + outer, outer)
            when(source < per_inner, lambda d=d, source=source: ag2_copy(j, d, source).wait_recv())
        for d in range(1, inner):
            ag1_copy(j, d, i).start()

    acc[...] = jnp.zeros_like(acc)

    def backward(j, k):
        from_inner = lax.rem(i - k + inner, inner)
        if k > 0:
            ag1_copy(j, k, from_inner).wait_recv()

        def one(n, carry):
            f = from_inner * per_part + n
            both = jnp.concatenate([res[j, f * tiles + t].astype(F32) for t in range(tiles)], 1)
            real, imag = both[:events], both[events:]
            left = jnp.concatenate(
                [jnp.concatenate([real, imag], 1), jnp.concatenate([imag, -real], 1)], 0
            ).astype(BF16)
            back = jnp.dot(left, g[f], preferred_element_type=F32)
            terms = back * s[j, f].astype(F32)
            total = terms[:8]
            for r in range(1, 2 * events // 8):
                total += terms[r * 8:(r + 1) * 8]
            acc[...] += total
            return carry

        lax.fori_loop(0, per_part, one, None)

    for k in range(inner):
        forward(0, k, True)
    for j in range(n_event):
        if j + 1 < n_event:
            beside = [functools.partial(forward, j + 1, k, False) for k in range(inner)]
            if j > 0:
                beside += [functools.partial(backward, j - 1, k) for k in range(inner)]
        else:
            beside = [functools.partial(backward, j - 1, k) for k in range(inner)] if j > 0 else []
        for n, stage in enumerate([stage1, stage2, stage3]):
            stage(j)
            if j == 0 and n < 2:
                for k in range(ahead + freqs // 2 + n, freqs, 2):
                    send_strain(k)
            if n < 2 or j + 1 < n_event:
                cut = len(beside) * (n + 1) // (3 if j + 1 < n_event else 2)
                for fn in beside[len(beside) * n // (3 if j + 1 < n_event else 2):cut]:
                    fn()
    for k in range(inner):
        backward(n_event - 1, k)

    local = acc[:, :cells]
    for c in range(1, comps):
        local += acc[:, c * cells:(c + 1) * cells]
    ends[0] = local

    def end_copy(d):
        return remote(ends.at[0], ends.at[d], end_s.at[d - 1], end_r.at[d - 1], at_event(-d))

    for d in range(1, n_event):
        end_copy(d).start()

    for j in range(1, n_event):
        for f in range(freqs):
            strain_copy(j, f).wait_send()
    for j in range(n_event):
        for d in range(1, inner):
            rs1_copy(j, d).wait_send()
            ag1_copy(j, d, i).wait_send()
        for d in range(1, outer):
            when(rs2_sends(d), lambda d=d, j=j: rs2_copy(j, d).wait_send())
            when(o < per_inner, lambda d=d, j=j: ag2_copy(j, d, o).wait_send())
    for d in range(1, n_event):
        end_copy(d).wait_recv()
    total = ends[0]
    for d in range(1, n_event):
        total += ends[d]
    total = scale_two * jnp.sum(total, axis=0, keepdims=True)
    width = cells // n_event
    mine = total[:, :width]
    for e in range(1, n_event):
        mine = jnp.where(y == e, total[:, e * width:(e + 1) * width], mine)
    out_ref[...] = mine
    for d in range(1, n_event):
        end_copy(d).wait_send()


def body(green, strain, perturb, pairs):
    freqs, recv = green.shape[0], green.shape[1]
    comps, cells = green.shape[3], green.shape[4]
    events = strain.shape[0]
    n_space = lax.axis_size("space")
    n_event = lax.axis_size("event")
    inner = 4
    outer = n_space // inner
    units = freqs * (recv // 128)
    per_inner = units // inner
    rows = 2 * comps
    flat_green = green.transpose(0, 1, 3, 2, 4).reshape(freqs, recv * rows, cells)
    flat_strain = strain.transpose(0, 1, 3, 2, 4).reshape(events * freqs * rows, cells)
    dma = pltpu.SemaphoreType.DMA
    wide = comps * cells
    hess = pl.pallas_call(
        functools.partial(kernel, n_space, n_event, inner, freqs, recv, comps, cells, events),
        out_shape=jax.ShapeDtypeStruct((1, cells // n_event), F32),
        in_specs=[
            pl.BlockSpec(memory_space=pl.ANY),
            pl.BlockSpec(memory_space=pl.ANY),
            pl.BlockSpec(memory_space=pltpu.VMEM),
            pl.BlockSpec(memory_space=pltpu.VMEM),
        ],
        out_specs=pl.BlockSpec(memory_space=pltpu.VMEM),
        scratch_shapes=[
            pltpu.VMEM((freqs, recv * rows, cells), BF16),
            pltpu.VMEM((events * freqs * rows, cells), BF16),
            pltpu.VMEM((recv * rows, cells), F32),
            pltpu.VMEM((events * freqs * rows, cells), F32),
            pltpu.VMEM((freqs, 2 * recv, wide), BF16),
            pltpu.VMEM((n_event, freqs, 2 * events, wide), BF16),
            pltpu.VMEM((n_event, units, 2 * events, 128), BF16),
            pltpu.VMEM((n_event, inner - 1, per_inner, 2 * events, 128), BF16),
            pltpu.VMEM((n_event, per_inner, 2 * events, 128), BF16),
            pltpu.VMEM((n_event, outer - 1, 2 * events, 128), BF16),
            pltpu.VMEM((n_event, units, 2 * events, 128), BF16),
            pltpu.VMEM((8, wide), F32),
            pltpu.VMEM((n_event, 8, cells), F32),
            dma((freqs + 1,)),
            dma((n_event - 1, freqs)),
            dma((n_event - 1, freqs)),
            dma((n_event, inner - 1)),
            dma((n_event, inner - 1)),
            dma((n_event, outer - 1)),
            dma((n_event, outer - 1)),
            dma((n_event, outer - 1)),
            dma((n_event, outer - 1)),
            dma((n_event, inner - 1)),
            dma((n_event, inner - 1)),
            dma((n_event - 1,)),
            dma((n_event - 1,)),
        ],
        compiler_params=pltpu.CompilerParams(
            collective_id=0, has_side_effects=True, vmem_limit_bytes=60 * 1024 * 1024
        ),
    )(flat_green, flat_strain, perturb.reshape(1, cells), pairs)
    return hess.reshape(-1)


def solution(mesh):
    in_specs = (
        P(None, "event", None, None, "space"),
        P("event", None, None, None, "space"),
        P("space"),
        P(None, "event"),
    )
    out_specs = P(("space", "event"))
    return jax.shard_map(body, mesh=mesh, in_specs=in_specs, out_specs=out_specs, check_vma=False)
```

```python
import functools
import math

import jax
import jax.numpy as jnp
from jax import lax
from jax.experimental import pallas as pl
from jax.experimental.pallas import tpu as pltpu
from jax.sharding import PartitionSpec as P

MESH = pl.DeviceIdType.MESH
F32 = jnp.float32
BF16 = jnp.bfloat16


def kernel(
    n_space, n_event, inner, freqs, recv, comps, cells, events,
    green_ref, strain_ref, perturb_ref, pairs_ref, out_ref,
    raw_green, raw_strain, wide_green, wide_strain, g, s, part, got1, half, got2, res, acc, ends,
    load_sem, strain_s, strain_r, rs1_s, rs1_r, rs2_s, rs2_r, ag2_s, ag2_r, ag1_s, ag1_r, end_s, end_r,
):
    outer = n_space // inner
    tiles = recv // 128
    per_inner = freqs * tiles // inner
    per_part = freqs // inner
    rows = 2 * comps
    scale_one = 1.0 / math.sqrt(12.0 * cells * n_space)
    scale_two = 1.0 / math.sqrt(12.0 * events * n_event * freqs * recv * n_event)

    me = lax.axis_index("space")
    y = lax.axis_index("event")
    i = lax.rem(me, inner)
    o = lax.div(me, inner)

    def at_event(d):
        return {"event": lax.rem(y + d + n_event, n_event)}

    def at_inner(d):
        return {"space": o * inner + lax.rem(i + d + inner, inner)}

    def at_outer(d):
        return {"space": lax.rem(o + d + outer, outer) * inner + i}

    def remote(src, dst, send, recv_, device):
        return pltpu.make_async_remote_copy(
            src_ref=src, dst_ref=dst, send_sem=send, recv_sem=recv_, device_id=device, device_id_type=MESH
        )

    def when(cond, fn):
        if per_inner == outer:
            fn()
        else:
            pl.when(cond)(fn)

    strain_load = pltpu.make_async_copy(strain_ref, raw_strain, load_sem.at[freqs])
    strain_load.start()

    def order(k):
        return lax.rem((i + 1) * per_part + k, freqs)

    def green_load(f):
        return pltpu.make_async_copy(green_ref.at[f], raw_green.at[f], load_sem.at[f])

    for k in range(freqs):
        green_load(order(k)).start()

    barrier = pltpu.get_barrier_semaphore()
    for d in range(1, n_event):
        pl.semaphore_signal(barrier, inc=1, device_id=at_event(d), device_id_type=MESH)
    for d in range(1, inner):
        pl.semaphore_signal(barrier, inc=1, device_id=at_inner(d), device_id_type=MESH)
    for d in range(1, outer):
        pl.semaphore_signal(barrier, inc=1, device_id=at_outer(d), device_id_type=MESH)

    strain_load.wait()
    wide_strain[...] = raw_strain[...].astype(F32)
    pl.semaphore_wait(barrier, n_event + inner + outer - 3)

    def strain_copy(j, f):
        return remote(s.at[0, f], s.at[j, f], strain_s.at[j - 1, f], strain_r.at[j - 1, f], at_event(-j))

    def arrange_strain(k, carry):
        f = order(k)
        for c in range(comps):
            pieces = [
                wide_strain[pl.ds(f * rows + 2 * c + q, events, stride=freqs * rows), :] for q in range(2)
            ]
            s[0, f, :, c * cells:(c + 1) * cells] = jnp.concatenate(pieces, 0).astype(BF16)
        return carry

    def send_strain(k):
        for j in range(1, n_event):
            strain_copy(j, order(k)).start()

    ahead = min(3, freqs)
    for k in range(ahead):
        arrange_strain(k, None)
        send_strain(k)

    perturb = jnp.concatenate([perturb_ref[...]] * comps, 1)

    def forward(j, k, arrange):
        def one(n, carry):
            f = order(k * per_part + n)
            if arrange:
                green_load(f).wait()
                wide_green[...] = raw_green[f].astype(F32)
                for c in range(comps):
                    for p in range(2):
                        g[f, p * recv:(p + 1) * recv, c * cells:(c + 1) * cells] = wide_green[
                            pl.ds(2 * c + p, recv, stride=rows), :
                        ].astype(BF16)
            if j > 0:
                for step in range(j, j + 1):
                    strain_copy(step, f).wait_recv()
            weighted = s[j, f].astype(F32) * perturb
            swapped = jnp.concatenate([-weighted[events:], weighted[:events]], 0)
            along = (((1,), (1,)), ((), ()))
            data = lax.dot_general(g[f, :recv], weighted.astype(BF16), along, preferred_element_type=F32)
            data += lax.dot_general(g[f, recv:], swapped.astype(BF16), along, preferred_element_type=F32)
            data = data.T.astype(BF16)
            for t in range(tiles):
                part[j, f * tiles + t] = data[:, t * 128:(t + 1) * 128]
            if arrange:
                step = k * per_part + n

                @pl.when(step + ahead < freqs)
                def _():
                    arrange_strain(step + ahead, None)
                    send_strain(step + ahead)
            return carry

        lax.fori_loop(0, per_part, one, None)
        if k < inner - 1:
            rs1_copy(j, k + 1).start()

    def rs1_copy(j, d):
        target = lax.rem(i + d, inner)
        return remote(
            part.at[j, pl.ds(target * per_inner, per_inner)], got1.at[j, d - 1],
            rs1_s.at[j, d - 1], rs1_r.at[j, d - 1], at_inner(d),
        )

    def rs2_copy(j, d):
        target = lax.rem(o + d, outer)
        return remote(half.at[j, target], got2.at[j, d - 1], rs2_s.at[j, d - 1], rs2_r.at[j, d - 1], at_outer(d))

    def rs2_sends(d):
        return lax.rem(o + d, outer) < per_inner

    def ag2_copy(j, d, t):
        spot = res.at[j, i * per_inner + t]
        return remote(spot, spot, ag2_s.at[j, d - 1], ag2_r.at[j, d - 1], at_outer(d))

    def ag1_copy(j, d, which):
        spot = res.at[j, pl.ds(which * per_inner, per_inner)]
        return remote(spot, spot, ag1_s.at[j, d - 1], ag1_r.at[j, d - 1], at_inner(d))

    def stage1(j):
        for d in range(1, inner):
            rs1_copy(j, d).wait_recv()
        for t in range(per_inner):
            total = part[j, i * per_inner + t].astype(F32)
            for d in range(1, inner):
                total += got1[j, d - 1, t].astype(F32)
            half[j, t] = total.astype(BF16)
        for d in range(1, outer):
            when(rs2_sends(d), lambda d=d: rs2_copy(j, d).start())

    def stage2(j):
        def reduce():
            for d in range(1, outer):
                rs2_copy(j, d).wait_recv()
            total = half[j, o].astype(F32)
            for d in range(1, outer):
                total += got2[j, d - 1].astype(F32)
            owner = lax.rem(y + j, n_event)
            mask = pairs_ref[pl.ds(pl.multiple_of(owner * events, 8), events), :].astype(F32)
            tile = lax.rem(o, tiles)
            chosen = mask[:, :128]
            for t in range(1, tiles):
                chosen = jnp.where(tile == t, mask[:, t * 128:(t + 1) * 128], chosen)
            chosen = jnp.concatenate([chosen, chosen], 0)
            res[j, i * per_inner + o] = (scale_one * total * chosen).astype(BF16)
            for d in range(1, outer):
                ag2_copy(j, d, o).start()

        when(o < per_inner, reduce)

    def stage3(j):
        for d in range(1, outer):
            source = lax.rem(o - d + outer, outer)
            when(source < per_inner, lambda d=d, source=source: ag2_copy(j, d, source).wait_recv())
        for d in range(1, inner):
            ag1_copy(j, d, i).start()

    acc[...] = jnp.zeros_like(acc)

    def backward(j, k):
        from_inner = lax.rem(i - k + inner, inner)
        if k > 0:
            ag1_copy(j, k, from_inner).wait_recv()

        def one(n, carry):
            f = from_inner * per_part + n
            both = jnp.concatenate([res[j, f * tiles + t].astype(F32) for t in range(tiles)], 1)
            real, imag = both[:events], both[events:]
            left = jnp.concatenate(
                [jnp.concatenate([real, imag], 1), jnp.concatenate([imag, -real], 1)], 0
            ).astype(BF16)
            back = jnp.dot(left, g[f], preferred_element_type=F32)
            terms = back * s[j, f].astype(F32)
            total = terms[:8]
            for r in range(1, 2 * events // 8):
                total += terms[r * 8:(r + 1) * 8]
            acc[...] += total
            return carry

        lax.fori_loop(0, per_part, one, None)

    for k in range(inner):
        forward(0, k, True)
    for j in range(n_event):
        last = j + 1 == n_event
        if not last:
            forward(j + 1, 0, False)
        stage1(j)
        if not last:
            forward(j + 1, 1, False)
        elif j > 0:
            backward(j - 1, 0)
            backward(j - 1, 1)
        stage2(j)
        if not last:
            forward(j + 1, 2, False)
        elif j > 0:
            backward(j - 1, 2)
            backward(j - 1, 3)
        stage3(j)
        if not last:
            forward(j + 1, 3, False)
            if j > 0:
                for k in range(inner):
                    backward(j - 1, k)
    for k in range(inner):
        backward(n_event - 1, k)

    local = acc[:, :cells]
    for c in range(1, comps):
        local += acc[:, c * cells:(c + 1) * cells]
    ends[0] = local

    def end_copy(d):
        return remote(ends.at[0], ends.at[d], end_s.at[d - 1], end_r.at[d - 1], at_event(-d))

    for d in range(1, n_event):
        end_copy(d).start()

    for j in range(1, n_event):
        for f in range(freqs):
            strain_copy(j, f).wait_send()
    for j in range(n_event):
        for d in range(1, inner):
            rs1_copy(j, d).wait_send()
            ag1_copy(j, d, i).wait_send()
        for d in range(1, outer):
            when(rs2_sends(d), lambda d=d, j=j: rs2_copy(j, d).wait_send())
            when(o < per_inner, lambda d=d, j=j: ag2_copy(j, d, o).wait_send())
    for d in range(1, n_event):
        end_copy(d).wait_recv()
    total = ends[0]
    for d in range(1, n_event):
        total += ends[d]
    total = scale_two * jnp.sum(total, axis=0, keepdims=True)
    width = cells // n_event
    mine = total[:, :width]
    for e in range(1, n_event):
        mine = jnp.where(y == e, total[:, e * width:(e + 1) * width], mine)
    out_ref[...] = mine
    for d in range(1, n_event):
        end_copy(d).wait_send()


def body(green, strain, perturb, pairs):
    freqs, recv = green.shape[0], green.shape[1]
    comps, cells = green.shape[3], green.shape[4]
    events = strain.shape[0]
    n_space = lax.axis_size("space")
    n_event = lax.axis_size("event")
    inner = 4
    outer = n_space // inner
    units = freqs * (recv // 128)
    per_inner = units // inner
    rows = 2 * comps
    flat_green = green.transpose(0, 1, 3, 2, 4).reshape(freqs, recv * rows, cells)
    flat_strain = strain.transpose(0, 1, 3, 2, 4).reshape(events * freqs * rows, cells)
    dma = pltpu.SemaphoreType.DMA
    wide = comps * cells
    hess = pl.pallas_call(
        functools.partial(kernel, n_space, n_event, inner, freqs, recv, comps, cells, events),
        out_shape=jax.ShapeDtypeStruct((1, cells // n_event), F32),
        in_specs=[
            pl.BlockSpec(memory_space=pl.ANY),
            pl.BlockSpec(memory_space=pl.ANY),
            pl.BlockSpec(memory_space=pltpu.VMEM),
            pl.BlockSpec(memory_space=pltpu.VMEM),
        ],
        out_specs=pl.BlockSpec(memory_space=pltpu.VMEM),
        scratch_shapes=[
            pltpu.VMEM((freqs, recv * rows, cells), BF16),
            pltpu.VMEM((events * freqs * rows, cells), BF16),
            pltpu.VMEM((recv * rows, cells), F32),
            pltpu.VMEM((events * freqs * rows, cells), F32),
            pltpu.VMEM((freqs, 2 * recv, wide), BF16),
            pltpu.VMEM((n_event, freqs, 2 * events, wide), BF16),
            pltpu.VMEM((n_event, units, 2 * events, 128), BF16),
            pltpu.VMEM((n_event, inner - 1, per_inner, 2 * events, 128), BF16),
            pltpu.VMEM((n_event, per_inner, 2 * events, 128), BF16),
            pltpu.VMEM((n_event, outer - 1, 2 * events, 128), BF16),
            pltpu.VMEM((n_event, units, 2 * events, 128), BF16),
            pltpu.VMEM((8, wide), F32),
            pltpu.VMEM((n_event, 8, cells), F32),
            dma((freqs + 1,)),
            dma((n_event - 1, freqs)),
            dma((n_event - 1, freqs)),
            dma((n_event, inner - 1)),
            dma((n_event, inner - 1)),
            dma((n_event, outer - 1)),
            dma((n_event, outer - 1)),
            dma((n_event, outer - 1)),
            dma((n_event, outer - 1)),
            dma((n_event, inner - 1)),
            dma((n_event, inner - 1)),
            dma((n_event - 1,)),
            dma((n_event - 1,)),
        ],
        compiler_params=pltpu.CompilerParams(
            collective_id=0, has_side_effects=True, vmem_limit_bytes=60 * 1024 * 1024
        ),
    )(flat_green, flat_strain, perturb.reshape(1, cells), pairs)
    return hess.reshape(-1)


def solution(mesh):
    in_specs = (
        P(None, "event", None, None, "space"),
        P("event", None, None, None, "space"),
        P("space"),
        P(None, "event"),
    )
    out_specs = P(("space", "event"))
    return jax.shard_map(body, mesh=mesh, in_specs=in_specs, out_specs=out_specs, check_vma=False)
```

```python
import functools
import math

import jax
import jax.numpy as jnp
from jax import lax
from jax.experimental import pallas as pl
from jax.experimental.pallas import tpu as pltpu
from jax.sharding import PartitionSpec as P

MESH = pl.DeviceIdType.MESH
F32 = jnp.float32
BF16 = jnp.bfloat16


def kernel(
    n_space, n_event, inner, freqs, recv, comps, cells, events,
    green_ref, strain_ref, perturb_ref, pairs_ref, out_ref,
    raw_green, raw_strain, wide_green, wide_strain, g, s, part, got1, half, got2, res, acc, ends,
    load_sem, strain_s, strain_r, rs1_s, rs1_r, rs2_s, rs2_r, ag2_s, ag2_r, ag1_s, ag1_r, end_s, end_r,
):
    outer = n_space // inner
    tiles = recv // 128
    per_inner = freqs * tiles // inner
    per_part = freqs // inner
    rows = 2 * comps
    scale_one = 1.0 / math.sqrt(12.0 * cells * n_space)
    scale_two = 1.0 / math.sqrt(12.0 * events * n_event * freqs * recv * n_event)

    me = lax.axis_index("space")
    y = lax.axis_index("event")
    i = lax.rem(me, inner)
    o = lax.div(me, inner)

    def at_event(d):
        return {"event": lax.rem(y + d + n_event, n_event)}

    def at_inner(d):
        return {"space": o * inner + lax.rem(i + d + inner, inner)}

    def at_outer(d):
        return {"space": lax.rem(o + d + outer, outer) * inner + i}

    def remote(src, dst, send, recv_, device):
        return pltpu.make_async_remote_copy(
            src_ref=src, dst_ref=dst, send_sem=send, recv_sem=recv_, device_id=device, device_id_type=MESH
        )

    def when(cond, fn):
        if per_inner == outer:
            fn()
        else:
            pl.when(cond)(fn)

    strain_load = pltpu.make_async_copy(strain_ref, raw_strain, load_sem.at[freqs])
    strain_load.start()

    def order(k):
        return lax.rem((i + 1) * per_part + k, freqs)

    def green_load(f):
        return pltpu.make_async_copy(green_ref.at[f], raw_green.at[f], load_sem.at[f])

    for k in range(freqs):
        green_load(order(k)).start()

    barrier = pltpu.get_barrier_semaphore()
    for d in range(1, n_event):
        pl.semaphore_signal(barrier, inc=1, device_id=at_event(d), device_id_type=MESH)
    for d in range(1, inner):
        pl.semaphore_signal(barrier, inc=1, device_id=at_inner(d), device_id_type=MESH)
    for d in range(1, outer):
        pl.semaphore_signal(barrier, inc=1, device_id=at_outer(d), device_id_type=MESH)

    strain_load.wait()
    wide_strain[...] = raw_strain[...].astype(F32)
    pl.semaphore_wait(barrier, n_event + inner + outer - 3)

    def strain_copy(j, f):
        return remote(s.at[0, f], s.at[j, f], strain_s.at[j - 1, f], strain_r.at[j - 1, f], at_event(-j))

    def arrange_strain(k, carry):
        f = order(k)
        for c in range(comps):
            pieces = [
                wide_strain[pl.ds(f * rows + 2 * c + q, events, stride=freqs * rows), :] for q in range(2)
            ]
            s[0, f, :, c * cells:(c + 1) * cells] = jnp.concatenate(pieces, 0).astype(BF16)
        return carry

    def send_strain(k):
        for j in range(1, n_event):
            strain_copy(j, order(k)).start()

    ahead = min(3, freqs)
    for k in range(ahead):
        arrange_strain(k, None)
        send_strain(k)

    perturb = jnp.concatenate([perturb_ref[...]] * comps, 1)

    def forward(j, first, count, arrange):
        def one(step, carry):
            f = order(step)
            if arrange:
                green_load(f).wait()
                wide_green[...] = raw_green[f].astype(F32)
                for c in range(comps):
                    for p in range(2):
                        g[f, p * recv:(p + 1) * recv, c * cells:(c + 1) * cells] = wide_green[
                            pl.ds(2 * c + p, recv, stride=rows), :
                        ].astype(BF16)
            if j > 0:
                strain_copy(j, f).wait_recv()
            weighted = s[j, f].astype(F32) * perturb
            swapped = jnp.concatenate([-weighted[events:], weighted[:events]], 0)
            along = (((1,), (1,)), ((), ()))
            data = lax.dot_general(g[f, :recv], weighted.astype(BF16), along, preferred_element_type=F32)
            data += lax.dot_general(g[f, recv:], swapped.astype(BF16), along, preferred_element_type=F32)
            data = data.T.astype(BF16)
            for t in range(tiles):
                part[j, f * tiles + t] = data[:, t * 128:(t + 1) * 128]
            if arrange:
                @pl.when(step + ahead < freqs)
                def _():
                    arrange_strain(step + ahead, None)
                    send_strain(step + ahead)

            @pl.when((lax.rem(step, per_part) == per_part - 1) & (step < freqs - per_part))
            def _():
                rs1_copy(j, lax.div(step, per_part) + 1).start()

            return carry

        lax.fori_loop(first * per_part, (first + count) * per_part, one, None)

    def rs1_copy(j, d):
        target = lax.rem(i + d, inner)
        return remote(
            part.at[j, pl.ds(target * per_inner, per_inner)], got1.at[j, d - 1],
            rs1_s.at[j, d - 1], rs1_r.at[j, d - 1], at_inner(d),
        )

    def rs2_copy(j, d):
        target = lax.rem(o + d, outer)
        return remote(half.at[j, target], got2.at[j, d - 1], rs2_s.at[j, d - 1], rs2_r.at[j, d - 1], at_outer(d))

    def rs2_sends(d):
        return lax.rem(o + d, outer) < per_inner

    def ag2_copy(j, d, t):
        spot = res.at[j, i * per_inner + t]
        return remote(spot, spot, ag2_s.at[j, d - 1], ag2_r.at[j, d - 1], at_outer(d))

    def ag1_copy(j, d, which):
        spot = res.at[j, pl.ds(which * per_inner, per_inner)]
        return remote(spot, spot, ag1_s.at[j, d - 1], ag1_r.at[j, d - 1], at_inner(d))

    def stage1(j):
        for d in range(1, inner):
            rs1_copy(j, d).wait_recv()
        for t in range(per_inner):
            total = part[j, i * per_inner + t].astype(F32)
            for d in range(1, inner):
                total += got1[j, d - 1, t].astype(F32)
            half[j, t] = total.astype(BF16)
        for d in range(1, outer):
            when(rs2_sends(d), lambda d=d: rs2_copy(j, d).start())

    def stage2(j):
        def reduce():
            for d in range(1, outer):
                rs2_copy(j, d).wait_recv()
            total = half[j, o].astype(F32)
            for d in range(1, outer):
                total += got2[j, d - 1].astype(F32)
            owner = lax.rem(y + j, n_event)
            mask = pairs_ref[pl.ds(pl.multiple_of(owner * events, 8), events), :].astype(F32)
            tile = lax.rem(o, tiles)
            chosen = mask[:, :128]
            for t in range(1, tiles):
                chosen = jnp.where(tile == t, mask[:, t * 128:(t + 1) * 128], chosen)
            chosen = jnp.concatenate([chosen, chosen], 0)
            res[j, i * per_inner + o] = (scale_one * total * chosen).astype(BF16)
            for d in range(1, outer):
                ag2_copy(j, d, o).start()

        when(o < per_inner, reduce)

    def stage3(j):
        for d in range(1, outer):
            source = lax.rem(o - d + outer, outer)
            when(source < per_inner, lambda d=d, source=source: ag2_copy(j, d, source).wait_recv())
        for d in range(1, inner):
            ag1_copy(j, d, i).start()

    acc[...] = jnp.zeros_like(acc)

    def backward(j, first, count):
        def one(step, carry):
            k = lax.div(step, per_part)
            from_inner = lax.rem(i - k + inner, inner)

            @pl.when((lax.rem(step, per_part) == 0) & (k > 0))
            def _():
                ag1_copy(j, k, from_inner).wait_recv()

            f = from_inner * per_part + lax.rem(step, per_part)
            both = jnp.concatenate([res[j, f * tiles + t].astype(F32) for t in range(tiles)], 1)
            real, imag = both[:events], both[events:]
            left = jnp.concatenate(
                [jnp.concatenate([real, imag], 1), jnp.concatenate([imag, -real], 1)], 0
            ).astype(BF16)
            back = jnp.dot(left, g[f], preferred_element_type=F32)
            terms = back * s[j, f].astype(F32)
            total = terms[:8]
            for r in range(1, 2 * events // 8):
                total += terms[r * 8:(r + 1) * 8]
            acc[...] += total
            return carry

        lax.fori_loop(first * per_part, (first + count) * per_part, one, None)

    forward(0, 0, inner, True)
    for j in range(n_event):
        last = j + 1 == n_event
        if not last:
            forward(j + 1, 0, 1, False)
        stage1(j)
        if not last:
            forward(j + 1, 1, 1, False)
        elif j > 0:
            backward(j - 1, 0, 2)
        stage2(j)
        if not last:
            forward(j + 1, 2, 1, False)
        elif j > 0:
            backward(j - 1, 2, 2)
        stage3(j)
        if not last:
            forward(j + 1, 3, 1, False)
            if j > 0:
                backward(j - 1, 0, inner)
    backward(n_event - 1, 0, inner)

    local = acc[:, :cells]
    for c in range(1, comps):
        local += acc[:, c * cells:(c + 1) * cells]
    ends[0] = local

    def end_copy(d):
        return remote(ends.at[0], ends.at[d], end_s.at[d - 1], end_r.at[d - 1], at_event(-d))

    for d in range(1, n_event):
        end_copy(d).start()

    for j in range(1, n_event):
        for f in range(freqs):
            strain_copy(j, f).wait_send()
    for j in range(n_event):
        for d in range(1, inner):
            rs1_copy(j, d).wait_send()
            ag1_copy(j, d, i).wait_send()
        for d in range(1, outer):
            when(rs2_sends(d), lambda d=d, j=j: rs2_copy(j, d).wait_send())
            when(o < per_inner, lambda d=d, j=j: ag2_copy(j, d, o).wait_send())
    for d in range(1, n_event):
        end_copy(d).wait_recv()
    total = ends[0]
    for d in range(1, n_event):
        total += ends[d]
    total = scale_two * jnp.sum(total, axis=0, keepdims=True)
    width = cells // n_event
    mine = total[:, :width]
    for e in range(1, n_event):
        mine = jnp.where(y == e, total[:, e * width:(e + 1) * width], mine)
    out_ref[...] = mine
    for d in range(1, n_event):
        end_copy(d).wait_send()


def body(green, strain, perturb, pairs):
    freqs, recv = green.shape[0], green.shape[1]
    comps, cells = green.shape[3], green.shape[4]
    events = strain.shape[0]
    n_space = lax.axis_size("space")
    n_event = lax.axis_size("event")
    inner = 4
    outer = n_space // inner
    units = freqs * (recv // 128)
    per_inner = units // inner
    rows = 2 * comps
    flat_green = green.transpose(0, 1, 3, 2, 4).reshape(freqs, recv * rows, cells)
    flat_strain = strain.transpose(0, 1, 3, 2, 4).reshape(events * freqs * rows, cells)
    dma = pltpu.SemaphoreType.DMA
    wide = comps * cells
    hess = pl.pallas_call(
        functools.partial(kernel, n_space, n_event, inner, freqs, recv, comps, cells, events),
        out_shape=jax.ShapeDtypeStruct((1, cells // n_event), F32),
        in_specs=[
            pl.BlockSpec(memory_space=pl.ANY),
            pl.BlockSpec(memory_space=pl.ANY),
            pl.BlockSpec(memory_space=pltpu.VMEM),
            pl.BlockSpec(memory_space=pltpu.VMEM),
        ],
        out_specs=pl.BlockSpec(memory_space=pltpu.VMEM),
        scratch_shapes=[
            pltpu.VMEM((freqs, recv * rows, cells), BF16),
            pltpu.VMEM((events * freqs * rows, cells), BF16),
            pltpu.VMEM((recv * rows, cells), F32),
            pltpu.VMEM((events * freqs * rows, cells), F32),
            pltpu.VMEM((freqs, 2 * recv, wide), BF16),
            pltpu.VMEM((n_event, freqs, 2 * events, wide), BF16),
            pltpu.VMEM((n_event, units, 2 * events, 128), BF16),
            pltpu.VMEM((n_event, inner - 1, per_inner, 2 * events, 128), BF16),
            pltpu.VMEM((n_event, per_inner, 2 * events, 128), BF16),
            pltpu.VMEM((n_event, outer - 1, 2 * events, 128), BF16),
            pltpu.VMEM((n_event, units, 2 * events, 128), BF16),
            pltpu.VMEM((8, wide), F32),
            pltpu.VMEM((n_event, 8, cells), F32),
            dma((freqs + 1,)),
            dma((n_event - 1, freqs)),
            dma((n_event - 1, freqs)),
            dma((n_event, inner - 1)),
            dma((n_event, inner - 1)),
            dma((n_event, outer - 1)),
            dma((n_event, outer - 1)),
            dma((n_event, outer - 1)),
            dma((n_event, outer - 1)),
            dma((n_event, inner - 1)),
            dma((n_event, inner - 1)),
            dma((n_event - 1,)),
            dma((n_event - 1,)),
        ],
        compiler_params=pltpu.CompilerParams(
            collective_id=0, has_side_effects=True, vmem_limit_bytes=60 * 1024 * 1024
        ),
    )(flat_green, flat_strain, perturb.reshape(1, cells), pairs)
    return hess.reshape(-1)


def solution(mesh):
    in_specs = (
        P(None, "event", None, None, "space"),
        P("event", None, None, None, "space"),
        P("space"),
        P(None, "event"),
    )
    out_specs = P(("space", "event"))
    return jax.shard_map(body, mesh=mesh, in_specs=in_specs, out_specs=out_specs, check_vma=False)
```

```python
import functools
import math

import jax
import jax.numpy as jnp
from jax import lax
from jax.experimental import pallas as pl
from jax.experimental.pallas import tpu as pltpu
from jax.sharding import PartitionSpec as P

MESH = pl.DeviceIdType.MESH
F32 = jnp.float32
BF16 = jnp.bfloat16


def kernel(
    n_space, n_event, inner, freqs, recv, comps, cells, events,
    green_ref, strain_ref, perturb_ref, pairs_ref, out_ref,
    raw_green, raw_strain, wide_green, wide_strain, g, s, part, got1, half, got2, res, acc, ends,
    load_sem, strain_s, strain_r, rs1_s, rs1_r, rs2_s, rs2_r, ag2_s, ag2_r, ag1_s, ag1_r, end_s, end_r,
):
    outer = n_space // inner
    tiles = recv // 128
    per_inner = freqs * tiles // inner
    per_part = freqs // inner
    rows = 2 * comps
    scale_one = 1.0 / math.sqrt(12.0 * cells * n_space)
    scale_two = 1.0 / math.sqrt(12.0 * events * n_event * freqs * recv * n_event)

    me = lax.axis_index("space")
    y = lax.axis_index("event")
    i = lax.rem(me, inner)
    o = lax.div(me, inner)

    def at_event(d):
        return {"event": lax.rem(y + d + n_event, n_event)}

    def at_inner(d):
        return {"space": o * inner + lax.rem(i + d + inner, inner)}

    def at_outer(d):
        return {"space": lax.rem(o + d + outer, outer) * inner + i}

    def remote(src, dst, send, recv_, device):
        return pltpu.make_async_remote_copy(
            src_ref=src, dst_ref=dst, send_sem=send, recv_sem=recv_, device_id=device, device_id_type=MESH
        )

    def when(cond, fn):
        if per_inner == outer:
            fn()
        else:
            pl.when(cond)(fn)

    strain_load = pltpu.make_async_copy(strain_ref, raw_strain, load_sem.at[freqs])
    strain_load.start()

    def order(k):
        return lax.rem((i + 1) * per_part + k, freqs)

    def green_load(f):
        return pltpu.make_async_copy(green_ref.at[f], raw_green.at[f], load_sem.at[f])

    for k in range(freqs):
        green_load(order(k)).start()

    barrier = pltpu.get_barrier_semaphore()
    for d in range(1, n_event):
        pl.semaphore_signal(barrier, inc=1, device_id=at_event(d), device_id_type=MESH)
    for d in range(1, inner):
        pl.semaphore_signal(barrier, inc=1, device_id=at_inner(d), device_id_type=MESH)
    for d in range(1, outer):
        pl.semaphore_signal(barrier, inc=1, device_id=at_outer(d), device_id_type=MESH)

    strain_load.wait()
    wide_strain[...] = raw_strain[...].astype(F32)
    pl.semaphore_wait(barrier, n_event + inner + outer - 3)

    def strain_copy(j, f):
        return remote(s.at[0, f], s.at[j, f], strain_s.at[j - 1, f], strain_r.at[j - 1, f], at_event(-j))

    def arrange_strain(k, carry):
        f = order(k)
        for c in range(comps):
            pieces = [
                wide_strain[pl.ds(f * rows + 2 * c + q, events, stride=freqs * rows), :] for q in range(2)
            ]
            s[0, f, :, c * cells:(c + 1) * cells] = jnp.concatenate(pieces, 0).astype(BF16)
        return carry

    def send_strain(k):
        for j in range(1, n_event):
            strain_copy(j, order(k)).start()

    ahead = min(3, freqs)
    for k in range(ahead):
        arrange_strain(k, None)
        send_strain(k)

    perturb = jnp.concatenate([perturb_ref[...]] * comps, 1)

    def forward(j, first, count, arrange):
        def one(step, carry):
            f = order(step)
            if arrange:
                green_load(f).wait()
                wide_green[...] = raw_green[f].astype(F32)
                for c in range(comps):
                    for p in range(2):
                        g[f, p * recv:(p + 1) * recv, c * cells:(c + 1) * cells] = wide_green[
                            pl.ds(2 * c + p, recv, stride=rows), :
                        ].astype(BF16)
            if j > 0:
                strain_copy(j, f).wait_recv()
            weighted = s[j, f].astype(F32) * perturb
            swapped = jnp.concatenate([-weighted[events:], weighted[:events]], 0)
            along = (((1,), (1,)), ((), ()))
            data = lax.dot_general(g[f, :recv], weighted.astype(BF16), along, preferred_element_type=F32)
            data += lax.dot_general(g[f, recv:], swapped.astype(BF16), along, preferred_element_type=F32)
            data = data.T.astype(BF16)
            for t in range(tiles):
                part[j, f * tiles + t] = data[:, t * 128:(t + 1) * 128]
            if arrange:
                @pl.when(step + ahead < freqs)
                def _():
                    arrange_strain(step + ahead, None)
                    send_strain(step + ahead)

            @pl.when((lax.rem(step, per_part) == per_part - 1) & (step < freqs - per_part))
            def _():
                rs1_copy(j, lax.div(step, per_part) + 1).start()

            return carry

        lax.fori_loop(first * per_part, (first + count) * per_part, one, None)

    def rs1_copy(j, d):
        target = lax.rem(i + d, inner)
        return remote(
            part.at[j, pl.ds(target * per_inner, per_inner)], got1.at[j, d - 1],
            rs1_s.at[j, d - 1], rs1_r.at[j, d - 1], at_inner(d),
        )

    def rs2_copy(j, d):
        target = lax.rem(o + d, outer)
        return remote(half.at[j, target], got2.at[j, d - 1], rs2_s.at[j, d - 1], rs2_r.at[j, d - 1], at_outer(d))

    def rs2_sends(d):
        return lax.rem(o + d, outer) < per_inner

    def ag2_copy(j, d, t):
        spot = res.at[j, i * per_inner + t]
        return remote(spot, spot, ag2_s.at[j, d - 1], ag2_r.at[j, d - 1], at_outer(d))

    def ag1_copy(j, d, which, t):
        spot = res.at[j, which * per_inner + t]
        return remote(spot, spot, ag1_s.at[j, d - 1, t], ag1_r.at[j, d - 1, t], at_inner(d))

    def stage1(j):
        for d in range(1, inner):
            rs1_copy(j, d).wait_recv()
        for t in range(per_inner):
            total = part[j, i * per_inner + t].astype(F32)
            for d in range(1, inner):
                total += got1[j, d - 1, t].astype(F32)
            half[j, t] = total.astype(BF16)
        for d in range(1, outer):
            when(rs2_sends(d), lambda d=d: rs2_copy(j, d).start())

    def stage2(j):
        def reduce():
            for d in range(1, outer):
                rs2_copy(j, d).wait_recv()
            total = half[j, o].astype(F32)
            for d in range(1, outer):
                total += got2[j, d - 1].astype(F32)
            owner = lax.rem(y + j, n_event)
            mask = pairs_ref[pl.ds(pl.multiple_of(owner * events, 8), events), :].astype(F32)
            tile = lax.rem(o, tiles)
            chosen = mask[:, :128]
            for t in range(1, tiles):
                chosen = jnp.where(tile == t, mask[:, t * 128:(t + 1) * 128], chosen)
            chosen = jnp.concatenate([chosen, chosen], 0)
            res[j, i * per_inner + o] = (scale_one * total * chosen).astype(BF16)
            for d in range(1, outer):
                ag2_copy(j, d, o).start()
            for d in range(1, inner):
                ag1_copy(j, d, i, o).start()

        when(o < per_inner, reduce)

    def stage3(j):
        for d in range(1, outer):
            source = lax.rem(o - d + outer, outer)

            def pass_on(d=d, source=source):
                ag2_copy(j, d, source).wait_recv()
                for e in range(1, inner):
                    ag1_copy(j, e, i, source).start()

            when(source < per_inner, pass_on)

    acc[...] = jnp.zeros_like(acc)

    def backward(j, first, count):
        def one(step, carry):
            k = lax.div(step, per_part)
            from_inner = lax.rem(i - k + inner, inner)

            n = lax.rem(step, per_part)

            @pl.when(k > 0)
            def _():
                for t in range(tiles):
                    ag1_copy(j, k, from_inner, n * tiles + t).wait_recv()

            f = from_inner * per_part + n
            both = jnp.concatenate([res[j, f * tiles + t].astype(F32) for t in range(tiles)], 1)
            real, imag = both[:events], both[events:]
            left = jnp.concatenate(
                [jnp.concatenate([real, imag], 1), jnp.concatenate([imag, -real], 1)], 0
            ).astype(BF16)
            back = jnp.dot(left, g[f], preferred_element_type=F32)
            terms = back * s[j, f].astype(F32)
            total = terms[:8]
            for r in range(1, 2 * events // 8):
                total += terms[r * 8:(r + 1) * 8]
            acc[...] += total
            return carry

        lax.fori_loop(first * per_part, (first + count) * per_part, one, None)

    forward(0, 0, inner, True)
    for j in range(n_event):
        last = j + 1 == n_event
        if not last:
            forward(j + 1, 0, 1, False)
        stage1(j)
        if not last:
            forward(j + 1, 1, 1, False)
        elif j > 0:
            backward(j - 1, 0, 2)
        stage2(j)
        if not last:
            forward(j + 1, 2, 1, False)
        elif j > 0:
            backward(j - 1, 2, 2)
        stage3(j)
        if not last:
            forward(j + 1, 3, 1, False)
            if j > 0:
                backward(j - 1, 0, inner)
    backward(n_event - 1, 0, inner)

    local = acc[:, :cells]
    for c in range(1, comps):
        local += acc[:, c * cells:(c + 1) * cells]
    ends[0] = local

    def end_copy(d):
        return remote(ends.at[0], ends.at[d], end_s.at[d - 1], end_r.at[d - 1], at_event(-d))

    for d in range(1, n_event):
        end_copy(d).start()

    for j in range(1, n_event):
        for f in range(freqs):
            strain_copy(j, f).wait_send()
    for j in range(n_event):
        for d in range(1, inner):
            rs1_copy(j, d).wait_send()
            for t in range(per_inner):
                ag1_copy(j, d, i, t).wait_send()
        for d in range(1, outer):
            when(rs2_sends(d), lambda d=d, j=j: rs2_copy(j, d).wait_send())
            when(o < per_inner, lambda d=d, j=j: ag2_copy(j, d, o).wait_send())
    for d in range(1, n_event):
        end_copy(d).wait_recv()
    total = ends[0]
    for d in range(1, n_event):
        total += ends[d]
    total = scale_two * jnp.sum(total, axis=0, keepdims=True)
    width = cells // n_event
    mine = total[:, :width]
    for e in range(1, n_event):
        mine = jnp.where(y == e, total[:, e * width:(e + 1) * width], mine)
    out_ref[...] = mine
    for d in range(1, n_event):
        end_copy(d).wait_send()


def body(green, strain, perturb, pairs):
    freqs, recv = green.shape[0], green.shape[1]
    comps, cells = green.shape[3], green.shape[4]
    events = strain.shape[0]
    n_space = lax.axis_size("space")
    n_event = lax.axis_size("event")
    inner = 4
    outer = n_space // inner
    units = freqs * (recv // 128)
    per_inner = units // inner
    rows = 2 * comps
    flat_green = green.transpose(0, 1, 3, 2, 4).reshape(freqs, recv * rows, cells)
    flat_strain = strain.transpose(0, 1, 3, 2, 4).reshape(events * freqs * rows, cells)
    dma = pltpu.SemaphoreType.DMA
    wide = comps * cells
    hess = pl.pallas_call(
        functools.partial(kernel, n_space, n_event, inner, freqs, recv, comps, cells, events),
        out_shape=jax.ShapeDtypeStruct((1, cells // n_event), F32),
        in_specs=[
            pl.BlockSpec(memory_space=pl.ANY),
            pl.BlockSpec(memory_space=pl.ANY),
            pl.BlockSpec(memory_space=pltpu.VMEM),
            pl.BlockSpec(memory_space=pltpu.VMEM),
        ],
        out_specs=pl.BlockSpec(memory_space=pltpu.VMEM),
        scratch_shapes=[
            pltpu.VMEM((freqs, recv * rows, cells), BF16),
            pltpu.VMEM((events * freqs * rows, cells), BF16),
            pltpu.VMEM((recv * rows, cells), F32),
            pltpu.VMEM((events * freqs * rows, cells), F32),
            pltpu.VMEM((freqs, 2 * recv, wide), BF16),
            pltpu.VMEM((n_event, freqs, 2 * events, wide), BF16),
            pltpu.VMEM((n_event, units, 2 * events, 128), BF16),
            pltpu.VMEM((n_event, inner - 1, per_inner, 2 * events, 128), BF16),
            pltpu.VMEM((n_event, per_inner, 2 * events, 128), BF16),
            pltpu.VMEM((n_event, outer - 1, 2 * events, 128), BF16),
            pltpu.VMEM((n_event, units, 2 * events, 128), BF16),
            pltpu.VMEM((8, wide), F32),
            pltpu.VMEM((n_event, 8, cells), F32),
            dma((freqs + 1,)),
            dma((n_event - 1, freqs)),
            dma((n_event - 1, freqs)),
            dma((n_event, inner - 1)),
            dma((n_event, inner - 1)),
            dma((n_event, outer - 1)),
            dma((n_event, outer - 1)),
            dma((n_event, outer - 1)),
            dma((n_event, outer - 1)),
            dma((n_event, inner - 1, per_inner)),
            dma((n_event, inner - 1, per_inner)),
            dma((n_event - 1,)),
            dma((n_event - 1,)),
        ],
        compiler_params=pltpu.CompilerParams(
            collective_id=0, has_side_effects=True, vmem_limit_bytes=60 * 1024 * 1024
        ),
    )(flat_green, flat_strain, perturb.reshape(1, cells), pairs)
    return hess.reshape(-1)


def solution(mesh):
    in_specs = (
        P(None, "event", None, None, "space"),
        P("event", None, None, None, "space"),
        P("space"),
        P(None, "event"),
    )
    out_specs = P(("space", "event"))
    return jax.shard_map(body, mesh=mesh, in_specs=in_specs, out_specs=out_specs, check_vma=False)
```

```python
import functools
import math

import jax
import jax.numpy as jnp
from jax import lax
from jax.experimental import pallas as pl
from jax.experimental.pallas import tpu as pltpu
from jax.sharding import PartitionSpec as P

MESH = pl.DeviceIdType.MESH
F32 = jnp.float32
BF16 = jnp.bfloat16


def kernel(
    n_space, n_event, inner, freqs, recv, comps, cells, events,
    green_ref, strain_ref, perturb_ref, pairs_ref, out_ref,
    raw_green, raw_strain, wide_green, wide_strain, g, s, part, got1, half, got2, res, acc, ends,
    load_sem, strain_s, strain_r, rs1_s, rs1_r, rs2_s, rs2_r, ag2_s, ag2_r, ag1_s, ag1_r, end_s, end_r,
):
    outer = n_space // inner
    tiles = recv // 128
    per_inner = freqs * tiles // inner
    per_part = freqs // inner
    rows = 2 * comps
    scale_one = 1.0 / math.sqrt(12.0 * cells * n_space)
    scale_two = 1.0 / math.sqrt(12.0 * events * n_event * freqs * recv * n_event)

    me = lax.axis_index("space")
    y = lax.axis_index("event")
    i = lax.rem(me, inner)
    o = lax.div(me, inner)

    def at_event(d):
        return {"event": lax.rem(y + d + n_event, n_event)}

    def at_inner(d):
        return {"space": o * inner + lax.rem(i + d + inner, inner)}

    def at_outer(d):
        return {"space": lax.rem(o + d + outer, outer) * inner + i}

    def remote(src, dst, send, recv_, device):
        return pltpu.make_async_remote_copy(
            src_ref=src, dst_ref=dst, send_sem=send, recv_sem=recv_, device_id=device, device_id_type=MESH
        )

    def when(cond, fn):
        if per_inner == outer:
            fn()
        else:
            pl.when(cond)(fn)

    strain_load = pltpu.make_async_copy(strain_ref, raw_strain, load_sem.at[freqs])
    strain_load.start()

    def order(k):
        return lax.rem((i + 1) * per_part + k, freqs)

    def green_load(f):
        return pltpu.make_async_copy(green_ref.at[f], raw_green.at[f], load_sem.at[f])

    for k in range(freqs):
        green_load(order(k)).start()

    barrier = pltpu.get_barrier_semaphore()
    for d in range(1, n_event):
        pl.semaphore_signal(barrier, inc=1, device_id=at_event(d), device_id_type=MESH)
    for d in range(1, inner):
        pl.semaphore_signal(barrier, inc=1, device_id=at_inner(d), device_id_type=MESH)
    for d in range(1, outer):
        pl.semaphore_signal(barrier, inc=1, device_id=at_outer(d), device_id_type=MESH)

    strain_load.wait()
    wide_strain[...] = raw_strain[...].astype(F32)
    pl.semaphore_wait(barrier, n_event + inner + outer - 3)

    def strain_copy(j, f):
        return remote(s.at[0, f], s.at[j, f], strain_s.at[j - 1, f], strain_r.at[j - 1, f], at_event(-j))

    def arrange_strain(k, carry):
        f = order(k)
        for c in range(comps):
            pieces = [
                wide_strain[pl.ds(f * rows + 2 * c + q, events, stride=freqs * rows), :] for q in range(2)
            ]
            s[0, f, :, c * cells:(c + 1) * cells] = jnp.concatenate(pieces, 0).astype(BF16)
        return carry

    def send_strain(k):
        for j in range(1, n_event):
            strain_copy(j, order(k)).start()

    ahead = min(3, freqs)
    for k in range(ahead):
        arrange_strain(k, None)
        send_strain(k)

    perturb = jnp.concatenate([perturb_ref[...]] * comps, 1)

    def forward(j, first, count, arrange):
        def one(step, carry):
            f = order(step)
            if arrange:
                green_load(f).wait()
                wide_green[...] = raw_green[f].astype(F32)
                for c in range(comps):
                    for p in range(2):
                        g[f, p * recv:(p + 1) * recv, c * cells:(c + 1) * cells] = wide_green[
                            pl.ds(2 * c + p, recv, stride=rows), :
                        ].astype(BF16)
            if j > 0:
                strain_copy(j, f).wait_recv()
            weighted = s[j, f].astype(F32) * perturb
            swapped = jnp.concatenate([-weighted[events:], weighted[:events]], 0)
            along = (((1,), (1,)), ((), ()))
            data = lax.dot_general(g[f, :recv], weighted.astype(BF16), along, preferred_element_type=F32)
            data += lax.dot_general(g[f, recv:], swapped.astype(BF16), along, preferred_element_type=F32)
            data = data.T.astype(BF16)
            for t in range(tiles):
                part[j, f * tiles + t] = data[:, t * 128:(t + 1) * 128]
            if arrange:
                @pl.when(step + ahead < freqs)
                def _():
                    arrange_strain(step + ahead, None)
                    send_strain(step + ahead)

            @pl.when((lax.rem(step, per_part) == per_part - 1) & (step < freqs - per_part))
            def _():
                rs1_copy(j, lax.div(step, per_part) + 1).start()

            return carry

        lax.fori_loop(first * per_part, (first + count) * per_part, one, None)

    def rs1_copy(j, d):
        target = lax.rem(i + d, inner)
        return remote(
            part.at[j, pl.ds(target * per_inner, per_inner)], got1.at[j, d - 1],
            rs1_s.at[j, d - 1], rs1_r.at[j, d - 1], at_inner(d),
        )

    def rs2_copy(j, d):
        target = lax.rem(o + d, outer)
        return remote(half.at[j, target], got2.at[j, d - 1], rs2_s.at[j, d - 1], rs2_r.at[j, d - 1], at_outer(d))

    def rs2_sends(d):
        return lax.rem(o + d, outer) < per_inner

    def ag2_copy(j, d, t):
        spot = res.at[j, i * per_inner + t]
        return remote(spot, spot, ag2_s.at[j, d - 1], ag2_r.at[j, d - 1], at_outer(d))

    def ag1_copy(j, d, which):
        spot = res.at[j, pl.ds(which * per_inner, per_inner)]
        return remote(spot, spot, ag1_s.at[j, d - 1], ag1_r.at[j, d - 1], at_inner(d))

    def stage1(j):
        for d in range(1, inner):
            rs1_copy(j, d).wait_recv()
        for t in range(per_inner):
            total = part[j, i * per_inner + t].astype(F32)
            for d in range(1, inner):
                total += got1[j, d - 1, t].astype(F32)
            half[j, t] = total.astype(BF16)
        for d in range(1, outer):
            when(rs2_sends(d), lambda d=d: rs2_copy(j, d).start())

    def stage2(j):
        def reduce():
            for d in range(1, outer):
                rs2_copy(j, d).wait_recv()
            total = half[j, o].astype(F32)
            for d in range(1, outer):
                total += got2[j, d - 1].astype(F32)
            owner = lax.rem(y + j, n_event)
            mask = pairs_ref[pl.ds(pl.multiple_of(owner * events, 8), events), :].astype(F32)
            tile = lax.rem(o, tiles)
            chosen = mask[:, :128]
            for t in range(1, tiles):
                chosen = jnp.where(tile == t, mask[:, t * 128:(t + 1) * 128], chosen)
            chosen = jnp.concatenate([chosen, chosen], 0)
            res[j, i * per_inner + o] = (scale_one * total * chosen).astype(BF16)
            for d in range(1, outer):
                ag2_copy(j, d, o).start()

        when(o < per_inner, reduce)

    def stage3(j):
        for d in range(1, outer):
            source = lax.rem(o - d + outer, outer)
            when(source < per_inner, lambda d=d, source=source: ag2_copy(j, d, source).wait_recv())
        for d in range(1, inner):
            ag1_copy(j, d, i).start()

    acc[...] = jnp.zeros_like(acc)

    def backward(j, first, count):
        def one(k, carry):
            from_inner = lax.rem(i - k + inner, inner)

            @pl.when(k > 0)
            def _():
                ag1_copy(j, k, from_inner).wait_recv()

            total = acc[...]
            for n in range(per_part):
                f = from_inner * per_part + n
                both = jnp.concatenate([res[j, f * tiles + t].astype(F32) for t in range(tiles)], 1)
                real, imag = both[:events], both[events:]
                left = jnp.concatenate(
                    [jnp.concatenate([real, imag], 1), jnp.concatenate([imag, -real], 1)], 0
                ).astype(BF16)
                back = jnp.dot(left, g[f], preferred_element_type=F32)
                terms = back * s[j, f].astype(F32)
                for r in range(2 * events // 8):
                    total += terms[r * 8:(r + 1) * 8]
            acc[...] = total
            return carry

        lax.fori_loop(first, first + count, one, None)

    forward(0, 0, inner, True)
    for j in range(n_event):
        last = j + 1 == n_event
        if not last:
            forward(j + 1, 0, 1, False)
        stage1(j)
        if not last:
            forward(j + 1, 1, 1, False)
        elif j > 0:
            backward(j - 1, 0, 2)
        stage2(j)
        if not last:
            forward(j + 1, 2, 1, False)
        elif j > 0:
            backward(j - 1, 2, 2)
        stage3(j)
        if not last:
            forward(j + 1, 3, 1, False)
            if j > 0:
                backward(j - 1, 0, inner)
    backward(n_event - 1, 0, inner)

    local = acc[:, :cells]
    for c in range(1, comps):
        local += acc[:, c * cells:(c + 1) * cells]
    ends[0] = local

    def end_copy(d):
        return remote(ends.at[0], ends.at[d], end_s.at[d - 1], end_r.at[d - 1], at_event(-d))

    for d in range(1, n_event):
        end_copy(d).start()

    for j in range(1, n_event):
        for f in range(freqs):
            strain_copy(j, f).wait_send()
    for j in range(n_event):
        for d in range(1, inner):
            rs1_copy(j, d).wait_send()
            ag1_copy(j, d, i).wait_send()
        for d in range(1, outer):
            when(rs2_sends(d), lambda d=d, j=j: rs2_copy(j, d).wait_send())
            when(o < per_inner, lambda d=d, j=j: ag2_copy(j, d, o).wait_send())
    for d in range(1, n_event):
        end_copy(d).wait_recv()
    total = ends[0]
    for d in range(1, n_event):
        total += ends[d]
    total = scale_two * jnp.sum(total, axis=0, keepdims=True)
    width = cells // n_event
    mine = total[:, :width]
    for e in range(1, n_event):
        mine = jnp.where(y == e, total[:, e * width:(e + 1) * width], mine)
    out_ref[...] = mine
    for d in range(1, n_event):
        end_copy(d).wait_send()


def body(green, strain, perturb, pairs):
    freqs, recv = green.shape[0], green.shape[1]
    comps, cells = green.shape[3], green.shape[4]
    events = strain.shape[0]
    n_space = lax.axis_size("space")
    n_event = lax.axis_size("event")
    inner = 4
    outer = n_space // inner
    units = freqs * (recv // 128)
    per_inner = units // inner
    rows = 2 * comps
    flat_green = green.transpose(0, 1, 3, 2, 4).reshape(freqs, recv * rows, cells)
    flat_strain = strain.transpose(0, 1, 3, 2, 4).reshape(events * freqs * rows, cells)
    dma = pltpu.SemaphoreType.DMA
    wide = comps * cells
    hess = pl.pallas_call(
        functools.partial(kernel, n_space, n_event, inner, freqs, recv, comps, cells, events),
        out_shape=jax.ShapeDtypeStruct((1, cells // n_event), F32),
        in_specs=[
            pl.BlockSpec(memory_space=pl.ANY),
            pl.BlockSpec(memory_space=pl.ANY),
            pl.BlockSpec(memory_space=pltpu.VMEM),
            pl.BlockSpec(memory_space=pltpu.VMEM),
        ],
        out_specs=pl.BlockSpec(memory_space=pltpu.VMEM),
        scratch_shapes=[
            pltpu.VMEM((freqs, recv * rows, cells), BF16),
            pltpu.VMEM((events * freqs * rows, cells), BF16),
            pltpu.VMEM((recv * rows, cells), F32),
            pltpu.VMEM((events * freqs * rows, cells), F32),
            pltpu.VMEM((freqs, 2 * recv, wide), BF16),
            pltpu.VMEM((n_event, freqs, 2 * events, wide), BF16),
            pltpu.VMEM((n_event, units, 2 * events, 128), BF16),
            pltpu.VMEM((n_event, inner - 1, per_inner, 2 * events, 128), BF16),
            pltpu.VMEM((n_event, per_inner, 2 * events, 128), BF16),
            pltpu.VMEM((n_event, outer - 1, 2 * events, 128), BF16),
            pltpu.VMEM((n_event, units, 2 * events, 128), BF16),
            pltpu.VMEM((8, wide), F32),
            pltpu.VMEM((n_event, 8, cells), F32),
            dma((freqs + 1,)),
            dma((n_event - 1, freqs)),
            dma((n_event - 1, freqs)),
            dma((n_event, inner - 1)),
            dma((n_event, inner - 1)),
            dma((n_event, outer - 1)),
            dma((n_event, outer - 1)),
            dma((n_event, outer - 1)),
            dma((n_event, outer - 1)),
            dma((n_event, inner - 1)),
            dma((n_event, inner - 1)),
            dma((n_event - 1,)),
            dma((n_event - 1,)),
        ],
        compiler_params=pltpu.CompilerParams(
            collective_id=0, has_side_effects=True, vmem_limit_bytes=60 * 1024 * 1024
        ),
    )(flat_green, flat_strain, perturb.reshape(1, cells), pairs)
    return hess.reshape(-1)


def solution(mesh):
    in_specs = (
        P(None, "event", None, None, "space"),
        P("event", None, None, None, "space"),
        P("space"),
        P(None, "event"),
    )
    out_specs = P(("space", "event"))
    return jax.shard_map(body, mesh=mesh, in_specs=in_specs, out_specs=out_specs, check_vma=False)
```
